768 devices in a mesh: dp: 8 (over x, core), tensor: 4 (over z_hi), expert: 24 (over y, z_lo).
Axes of the slice: x: 4, y: 8, z: 12 (z_hi: 4, z_lo: 3; z = z_hi * 3 + z_lo), core: 2. Of those that a mesh axis runs over, the one named last changes fastest.
Arguments:
- attn_heads: bfloat16 [8, 24, 24, 2560], P('dp', None, 'expert', 'tensor'), may hold values from -13 to 13, as said below
- out_proj: bfloat16 [2560, 5120], P('tensor'), may hold values from -0.125 to 0.125
- norm_gain: float32 [5120], replicated, may hold values from 0.5 to 2
- router: bfloat16 [5120, 24], replicated, may hold values from -0.15625 to 0.15625
- expert_ids: int32 [8, 24, 24], P('dp', 'tensor', 'expert'), may hold values from 0 to 23, as said below
- w_gate: bfloat16 [24, 5120, 4096], P('expert', None, ('dp', 'tensor')), may hold values from -0.078125 to 0.078125
- w_up: bfloat16 [24, 5120, 4096], P('expert', None, ('dp', 'tensor')), may hold values from -0.078125 to 0.078125
- w_down: bfloat16 [24, 4096, 5120], P('expert', ('dp', 'tensor')), may hold values from -0.1875 to 0.1875
Outputs:
- expert_out: bfloat16 [8, 24, 24, 5120], P('dp', 'tensor', 'expert')
The draws below stay inside these ranges and needn't reach their ends.
Inputs may be any that keep to these rules, and one draw needn't show every extreme that they name: `attn_heads`: values are those of a random draw, possibly with a component shared by all tokens, times a factor for each token. `expert_ids`: among the tokens of one device, at most 2 name the same expert, and some device of each dp and tensor index has exactly 2 naming one. Among the tokens of the 24 devices that share a dp index and a tensor index, at most 8 name the same expert, and in every such group one expert is named exactly 8 times.
All inputs are finite; a program needn't handle non-finite values.
Results may differ from the reference program's by a relative error of at most 0.0095.
Values may be sent and summed in bfloat16 or wider, within the bound.
No kernel may reach another device: no remote copies, remote signals or barrier semaphores. Data moves between devices by JAX's collectives and lax.ppermute only.
A program may use at most 32 MiB of HBM per device.

```python
import math
import jax
import jax.numpy as jnp
from jax import lax

D = 5120
HD = 2560
FF = 4096
TOK_DEV = 6
SEND_CAP = 2
EXPERTS = 24
RECV_CAP = 8
TOKENS = 4608
N_DP = 8
N_TENSOR = 4
N_EXPERT = 24


def slab_routes(slab_key):
    total = N_EXPERT * TOK_DEV
    key_order, key_steps, key_source, key_slots = jax.random.split(slab_key, 4)
    expert_order = jax.random.permutation(key_order, N_EXPERT)
    extra = RECV_CAP - TOK_DEV
    step_sizes = jax.random.randint(key_steps, (N_EXPERT // 2,), 0, extra + 1)
    step_sizes = step_sizes.at[0].set(extra)
    run_sizes = jnp.stack([TOK_DEV + step_sizes, TOK_DEV - step_sizes], axis=1).reshape(-1)
    run_ends = jnp.cumsum(run_sizes)
    position = jnp.arange(total, dtype=jnp.int32)
    run_index = jnp.sum((run_ends[None, :] <= position[:, None]).astype(jnp.int32), axis=1)
    labels = expert_order[run_index]
    group_index = position // SEND_CAP
    source = group_index % N_EXPERT
    slot_pos = group_index // N_EXPERT * SEND_CAP + position % SEND_CAP
    source = jax.random.permutation(key_source, N_EXPERT)[source]

    def shuffle_one(shuffle_key):
        return jax.random.permutation(shuffle_key, TOK_DEV)
    shuffles = jax.vmap(shuffle_one)(jax.random.split(key_slots, N_EXPERT))
    slot_pos = shuffles[source, slot_pos]
    route_table = jnp.zeros((TOK_DEV, N_EXPERT), jnp.int32).at[slot_pos, source].set(labels)
    return route_table


def draw_expert_ids(key, part):
    key = jax.random.fold_in(key, 7)
    slab_keys = jax.random.split(key, N_DP * N_TENSOR)
    tables = jax.vmap(slab_routes)(slab_keys)
    return tables.reshape(N_DP, N_TENSOR * TOK_DEV, N_EXPERT)


def draw_attn_heads(key, part):
    key = jax.random.fold_in(key, 11)
    key_rows, key_base = jax.random.split(key, 2)
    shape = (N_DP, N_TENSOR * TOK_DEV, N_EXPERT, HD)
    factors = jnp.exp(jax.random.uniform(key_rows, (N_DP, N_TENSOR * TOK_DEV, N_EXPERT, 1), jnp.float32, -1.15, 1.15))
    base = jnp.clip(jax.random.normal(key_base, shape, jnp.float32), -4.0, 4.0)
    return (base * factors).astype(jnp.bfloat16)


def shard_levels(stream_key, shape, pieces, least, top_value):
    level, own = 1.0, jax.random.fold_in(stream_key, 6)
    for dim, parts in pieces:
        draws = jnp.exp(jax.random.uniform(jax.random.fold_in(own, dim), (parts,), jnp.float32, least / len(pieces), top_value / len(pieces)))
        level = level * jnp.repeat(draws, shape[dim] // parts).reshape([-1 if axis == dim else 1 for axis in range(len(shape))])
    return level


def bell_draw(key, shape, scale, most, cuts=(), kind=jnp.bfloat16):
    entries = jax.random.normal(key, shape, jnp.float32) * scale
    if len(cuts) > 0:
        entries = shard_levels(key, shape, cuts, -0.22, 0.18) * entries
    return jnp.clip(entries, min=-most, max=most).astype(kind)


def setup_inputs(seed: int = 0) -> dict:
    seeds = jax.random.split(jax.random.key(seed), 9)
    return {
        "attn_heads": draw_attn_heads(jax.random.fold_in(seeds[8], 71), 0),
        "out_proj": bell_draw(seeds[1], (HD, D), HD ** -0.5, 0.125, ((0, 4),)),
        "norm_gain": jnp.clip(jnp.exp(jax.random.uniform(seeds[2], (D,), jnp.float32, math.log(0.5), math.log(2.0))), 0.5, 2.0),
        "router": bell_draw(seeds[3], (D, EXPERTS), (D // 4) ** -0.5, 0.15625),
        "expert_ids": draw_expert_ids(jax.random.fold_in(seeds[8], 71), 0),
        "w_gate": bell_draw(seeds[5], (EXPERTS, D, FF), D ** -0.5, 0.078125, ((0, 24), (2, 32))),
        "w_up": bell_draw(seeds[6], (EXPERTS, D, FF), D ** -0.5, 0.078125, ((0, 24), (2, 32))),
        "w_down": bell_draw(seeds[7], (EXPERTS, FF, D), (FF // 4) ** -0.5, 0.1875, ((0, 24), (1, 32))),
    }


def reference(attn_heads, out_proj, norm_gain, router, expert_ids, w_gate, w_up, w_down):
    head_rows = attn_heads.reshape(-1, attn_heads.shape[-1])
    attended = jnp.dot(head_rows, out_proj, preferred_element_type=jnp.float32)
    inverse = lax.rsqrt(lax.optimization_barrier(jnp.mean(attended * attended, axis=-1, keepdims=True)) + 1e-05)
    normed = attended * inverse * norm_gain
    router_logits = jnp.dot(normed.astype(jnp.bfloat16), router, preferred_element_type=jnp.float32)
    chosen_ids = expert_ids.reshape(-1).astype(jnp.int32)
    picked = jnp.take_along_axis(router_logits, chosen_ids[:, None], axis=1)[:, 0]
    router_score = jax.nn.sigmoid(picked)
    routed = (normed * router_score[:, None]).astype(jnp.bfloat16)
    most_rows = RECV_CAP * N_DP * N_TENSOR

    def one_expert(index):
        matches = chosen_ids == index
        found = jnp.nonzero(matches, size=most_rows, fill_value=0)[0].astype(jnp.int32)
        valid = jnp.arange(most_rows, dtype=jnp.int32) < jnp.sum(matches.astype(jnp.int32))
        rows_in = routed[found]
        gate_value = jnp.dot(rows_in, w_gate[index], preferred_element_type=jnp.float32)
        up_value = jnp.dot(rows_in, w_up[index], preferred_element_type=jnp.float32)
        hidden = (jax.nn.silu(gate_value) * up_value).astype(jnp.bfloat16)
        out_rows = jnp.dot(hidden, w_down[index], preferred_element_type=jnp.float32).astype(jnp.bfloat16)
        out_rows = jnp.where(valid[:, None], out_rows, jnp.zeros_like(out_rows))
        return (found, out_rows)
    found_all, out_all = lax.map(one_expert, jnp.arange(EXPERTS, dtype=jnp.int32))
    result = jnp.zeros((TOKENS, D), jnp.bfloat16)
    result = result.at[found_all.reshape(-1)].add(out_all.reshape(-1, D))
    return result.reshape(expert_ids.shape + (D,))
```

```python
import jax
import jax.numpy as jnp
from jax import lax
from jax.sharding import Mesh, PartitionSpec as P

BF = jnp.bfloat16
F32 = jnp.float32
LANES = 128


def exchange(value, axis):
    return lax.all_to_all(value, axis, split_axis=0, concat_axis=0, tiled=True)


def spread(value, axis):
    count = lax.axis_size(axis)
    return exchange(jnp.broadcast_to(value[None], (count,) + value.shape), axis)


def total_over(partial, axis):
    return jnp.sum(exchange(partial.astype(BF), axis).astype(F32), axis=0)


def on_device(attn_heads, out_proj, norm_gain, router, expert_ids, w_gate, w_up, w_down):
    tensor_count = lax.axis_size("tensor")
    x_count = lax.axis_size("x")
    expert_axes = ("y", "w")
    expert_count = lax.axis_size(expert_axes)
    swap = [(0, 1), (1, 0)]
    head_rows = attn_heads.reshape(-1, attn_heads.shape[-1])
    tok_rows = head_rows.shape[0] // tensor_count
    width = out_proj.shape[1]
    send_cap = max(2, tok_rows // (expert_count // 2))
    recv_cap = min(tok_rows + max(2, tok_rows // 5), send_cap * (expert_count - 2) + 2)
    slots = expert_count * send_cap

    partial = jnp.dot(head_rows, out_proj, preferred_element_type=F32)
    attended = total_over(partial.reshape(tensor_count, tok_rows, width), "tensor")

    inverse = lax.rsqrt(jnp.mean(attended * attended, axis=-1, keepdims=True) + 1e-05)
    normed = attended * inverse * norm_gain
    router_logits = jnp.dot(normed.astype(BF), router, preferred_element_type=F32)
    chosen_ids = expert_ids.reshape(-1)
    expert_index = jnp.arange(expert_count, dtype=jnp.int32)
    member_mask = chosen_ids[:, None] == expert_index[None, :]
    router_score = jax.nn.sigmoid(jnp.sum(jnp.where(member_mask, router_logits, 0.0), axis=1))
    routed = (normed * router_score[:, None]).astype(BF)

    same = chosen_ids[:, None] == chosen_ids[None, :]
    earlier = jnp.arange(tok_rows)[None, :] < jnp.arange(tok_rows)[:, None]
    rank_within = jnp.sum((same & earlier).astype(jnp.int32), axis=1)
    slot_index = chosen_ids * send_cap + rank_within
    slot_range = jnp.arange(slots, dtype=jnp.int32)
    placing = (slot_range[:, None] == slot_index[None, :]).astype(BF)
    flagged = jnp.concatenate([routed, jnp.ones((tok_rows, LANES), BF)], axis=1)
    outgoing = jnp.dot(placing, flagged, preferred_element_type=F32).astype(BF)
    arrived = exchange(outgoing.reshape(expert_count, send_cap, width + LANES), expert_axes)
    arrived = arrived.reshape(slots, width + LANES)

    filled = arrived[:, width].astype(F32)
    before = slot_range[:, None] < slot_range[None, :]
    position = jnp.sum(jnp.where(before, filled[:, None], 0.0), axis=0).astype(jnp.int32)
    position = jnp.where(filled > 0.5, position, -1)
    selector = (jnp.arange(recv_cap, dtype=jnp.int32)[:, None] == position[None, :]).astype(BF)
    compact = jnp.dot(selector, arrived[:, :width], preferred_element_type=F32).astype(BF)

    rows = spread(compact, "tensor").reshape(tensor_count * recv_cap, width)
    rows = spread(rows, "x").reshape(x_count * tensor_count * recv_cap, width)
    other_rows = lax.ppermute(rows, "core", swap)

    def expert_part(block):
        gate_value = jnp.dot(block, w_gate[0], preferred_element_type=F32)
        up_value = jnp.dot(block, w_up[0], preferred_element_type=F32)
        hidden = (jax.nn.silu(gate_value) * up_value).astype(BF)
        return jnp.dot(hidden, w_down[0], preferred_element_type=F32)

    own_sum = expert_part(rows)
    other_sum = expert_part(other_rows)
    pair_sum = own_sum + lax.ppermute(other_sum.astype(BF), "core", swap).astype(F32)
    plane_sum = total_over(pair_sum.reshape(x_count, tensor_count * recv_cap, width), "x")
    expert_rows = total_over(plane_sum.reshape(tensor_count, recv_cap, width), "tensor").astype(BF)

    back = jnp.dot(selector.T, expert_rows, preferred_element_type=F32).astype(BF)
    returned = exchange(back.reshape(expert_count, send_cap, width), expert_axes)
    combined = jnp.dot(placing.T, returned.reshape(slots, width), preferred_element_type=F32)
    return combined.astype(BF).reshape(1, tok_rows, 1, width)


def solution(mesh):
    dp, tensor, expert = (mesh.shape[name] for name in ("dp", "tensor", "expert"))
    fine = Mesh(
        mesh.devices.reshape(dp // 2, 2, tensor, expert // 3, 3), ("x", "core", "tensor", "y", "w")
    )
    dp_axes, expert_axes = ("x", "core"), ("y", "w")
    in_specs = (
        P(dp_axes, None, expert_axes, "tensor"),
        P("tensor", None),
        P(),
        P(),
        P(dp_axes, "tensor", expert_axes),
        P(expert_axes, None, (*dp_axes, "tensor")),
        P(expert_axes, None, (*dp_axes, "tensor")),
        P(expert_axes, (*dp_axes, "tensor"), None),
    )
    out_specs = P(dp_axes, "tensor", expert_axes, None)
    return jax.shard_map(
        on_device, mesh=fine, in_specs=in_specs, out_specs=out_specs, check_vma=False
    )
```

```python
import jax
import jax.numpy as jnp
from jax import lax
from jax.experimental import pallas as pl
from jax.experimental.pallas import tpu as pltpu
from jax.sharding import Mesh, PartitionSpec as P

BF = jnp.bfloat16
F32 = jnp.float32
LANES = 128


def exchange(value, axis):
    return lax.all_to_all(value, axis, split_axis=0, concat_axis=0, tiled=True)


def spread(value, axis):
    count = lax.axis_size(axis)
    return exchange(jnp.broadcast_to(value[None], (count,) + value.shape), axis)


def total_of(parts):
    total = parts[0].astype(F32)
    for index in range(1, parts.shape[0]):
        total = total + parts[index].astype(F32)
    return total


def in_vmem(value):
    return pltpu.with_memory_space_constraint(value, pltpu.VMEM)


def local_call(kernel, shape, *operands):
    whole = pl.BlockSpec(memory_space=pltpu.VMEM)
    return pl.pallas_call(
        kernel,
        out_shape=pltpu.VMEM(shape, BF),
        in_specs=[whole] * len(operands),
        out_specs=whole,
        compiler_params=pltpu.CompilerParams(vmem_limit_bytes=12 << 20),
    )(*operands)


def project_kernel(heads_ref, weight_ref, out_ref):
    out_ref[...] = jnp.dot(heads_ref[...], weight_ref[...], preferred_element_type=F32).astype(BF)


def project(heads, weight):
    rows, depth = heads.shape
    width = weight.shape[1]
    block = 512
    return pl.pallas_call(
        project_kernel,
        grid=(width // block,),
        out_shape=pltpu.VMEM((rows, width), BF),
        in_specs=[
            pl.BlockSpec((rows, depth), lambda i: (0, 0)),
            pl.BlockSpec((depth, block), lambda i: (0, i)),
        ],
        out_specs=pl.BlockSpec((rows, block), lambda i: (0, i)),
    )(in_vmem(heads), pltpu.with_memory_space_constraint(weight, pltpu.HBM))


def hidden_of(rows_ref, gate_ref, up_ref):
    rows = rows_ref[...]
    gate_value = jnp.dot(rows, gate_ref[...], preferred_element_type=F32)
    up_value = jnp.dot(rows, up_ref[...], preferred_element_type=F32)
    return (jax.nn.silu(gate_value) * up_value).astype(BF)


def hidden_kernel(rows_ref, gate_ref, up_ref, out_ref):
    out_ref[...] = hidden_of(rows_ref, gate_ref, up_ref)


def expert_kernel(rows_ref, gate_ref, up_ref, down_ref, out_ref):
    hidden = hidden_of(rows_ref, gate_ref, up_ref)
    out_ref[...] = jnp.dot(hidden, down_ref[...], preferred_element_type=F32).astype(BF)


def down_add_kernel(hidden_ref, down_ref, arrived_ref, out_ref):
    own = jnp.dot(hidden_ref[...], down_ref[...], preferred_element_type=F32)
    out_ref[...] = (own + arrived_ref[...].astype(F32)).astype(BF)


def on_device(attn_heads, out_proj, norm_gain, router, expert_ids, w_gate, w_up, w_down):
    tensor_count = lax.axis_size("tensor")
    x_count = lax.axis_size("x")
    expert_axes = ("y", "w")
    expert_count = lax.axis_size(expert_axes)
    swap = [(0, 1), (1, 0)]
    head_rows = attn_heads.reshape(-1, attn_heads.shape[-1])
    tok_rows = head_rows.shape[0] // tensor_count
    width = out_proj.shape[1]
    send_cap = max(2, tok_rows // (expert_count // 2))
    recv_cap = min(tok_rows + max(2, tok_rows // 5), send_cap * (expert_count - 2) + 2)
    slots = expert_count * send_cap

    pad_rows = -(-tok_rows // 8) * 8
    heads = head_rows.reshape(tensor_count, tok_rows, -1)
    heads = jnp.pad(heads, ((0, 0), (0, pad_rows - tok_rows), (0, 0)))
    partial = project(heads.reshape(tensor_count * pad_rows, -1), out_proj)
    partial = exchange(partial.reshape(tensor_count, pad_rows, width), "tensor")
    attended = total_of(partial)[:tok_rows]

    inverse = lax.rsqrt(jnp.mean(attended * attended, axis=-1, keepdims=True) + 1e-05)
    normed = attended * inverse * norm_gain
    router_logits = jnp.dot(normed.astype(BF), router, preferred_element_type=F32)
    chosen_ids = expert_ids.reshape(-1)
    expert_index = jnp.arange(expert_count, dtype=jnp.int32)
    member_mask = chosen_ids[:, None] == expert_index[None, :]
    router_score = jax.nn.sigmoid(jnp.sum(jnp.where(member_mask, router_logits, 0.0), axis=1))
    routed = (normed * router_score[:, None]).astype(BF)

    same = chosen_ids[:, None] == chosen_ids[None, :]
    earlier = jnp.arange(tok_rows)[None, :] < jnp.arange(tok_rows)[:, None]
    rank_within = jnp.sum((same & earlier).astype(jnp.int32), axis=1)
    slot_index = chosen_ids * send_cap + rank_within
    slot_range = jnp.arange(slots, dtype=jnp.int32)
    placing = (slot_range[:, None] == slot_index[None, :]).astype(BF)
    flagged = jnp.concatenate([routed, jnp.ones((tok_rows, LANES), BF)], axis=1)
    outgoing = jnp.dot(placing, flagged, preferred_element_type=F32).astype(BF)
    arrived = exchange(outgoing.reshape(expert_count, send_cap, width + LANES), expert_axes)
    arrived = arrived.reshape(slots, width + LANES)

    filled = arrived[:, width].astype(F32)
    before = slot_range[:, None] < slot_range[None, :]
    position = jnp.sum(jnp.where(before, filled[:, None], 0.0), axis=0).astype(jnp.int32)
    position = jnp.where(filled > 0.5, position, -1)
    selector = (jnp.arange(recv_cap, dtype=jnp.int32)[:, None] == position[None, :]).astype(BF)
    compact = jnp.dot(selector, arrived[:, :width], preferred_element_type=F32).astype(BF)

    rows = spread(compact, "tensor").reshape(tensor_count * recv_cap, width)
    rows = spread(rows, "x").reshape(x_count * tensor_count * recv_cap, width)
    other_rows = lax.ppermute(rows, "core", swap)

    gate, up, down = w_gate[0], w_up[0], w_down[0]
    units = gate.shape[1]
    own_hidden = local_call(hidden_kernel, (rows.shape[0], units), rows, gate, up)
    own_hidden, other_rows = lax.optimization_barrier((own_hidden, other_rows))
    other_sum = local_call(expert_kernel, rows.shape, other_rows, gate, up, down)
    other_sum = lax.ppermute(other_sum, "core", swap)
    pair_sum = local_call(down_add_kernel, rows.shape, own_hidden, down, other_sum)
    plane_sum = total_of(
        exchange(pair_sum.reshape(x_count, tensor_count * recv_cap, width), "x")
    ).astype(BF)
    expert_rows = total_of(
        exchange(plane_sum.reshape(tensor_count, recv_cap, width), "tensor")
    ).astype(BF)

    back = jnp.dot(selector.T, expert_rows, preferred_element_type=F32).astype(BF)
    returned = exchange(back.reshape(expert_count, send_cap, width), expert_axes)
    combined = jnp.dot(placing.T, returned.reshape(slots, width), preferred_element_type=F32)
    return combined.astype(BF).reshape(1, tok_rows, 1, width)


def solution(mesh):
    dp, tensor, expert = (mesh.shape[name] for name in ("dp", "tensor", "expert"))
    fine = Mesh(
        mesh.devices.reshape(dp // 2, 2, tensor, expert // 3, 3), ("x", "core", "tensor", "y", "w")
    )
    dp_axes, expert_axes = ("x", "core"), ("y", "w")
    in_specs = (
        P(dp_axes, None, expert_axes, "tensor"),
        P("tensor", None),
        P(),
        P(),
        P(dp_axes, "tensor", expert_axes),
        P(expert_axes, None, (*dp_axes, "tensor")),
        P(expert_axes, None, (*dp_axes, "tensor")),
        P(expert_axes, (*dp_axes, "tensor"), None),
    )
    out_specs = P(dp_axes, "tensor", expert_axes, None)
    return jax.shard_map(
        on_device, mesh=fine, in_specs=in_specs, out_specs=out_specs, check_vma=False
    )
```

```python
import functools

import jax
import jax.numpy as jnp
from jax import lax
from jax.experimental import pallas as pl
from jax.experimental.pallas import tpu as pltpu
from jax.sharding import Mesh, PartitionSpec as P

BF = jnp.bfloat16
F32 = jnp.float32
LANES = 128


def exchange(value, axis):
    return lax.all_to_all(value, axis, split_axis=0, concat_axis=0, tiled=True)


def spread(value, axis):
    count = lax.axis_size(axis)
    return exchange(jnp.broadcast_to(value[None], (count,) + value.shape), axis)


def total_of(parts):
    total = parts[0].astype(F32)
    for index in range(1, parts.shape[0]):
        total = total + parts[index].astype(F32)
    return total


def in_vmem(value):
    return pltpu.with_memory_space_constraint(value, pltpu.VMEM)


def local_call(kernel, shape, *operands):
    whole = pl.BlockSpec(memory_space=pltpu.VMEM)
    scalars = pl.BlockSpec(memory_space=pltpu.SMEM)
    return pl.pallas_call(
        kernel,
        out_shape=pltpu.VMEM(shape, BF),
        in_specs=[whole if operand.dtype == BF else scalars for operand in operands],
        out_specs=whole,
        compiler_params=pltpu.CompilerParams(vmem_limit_bytes=12 << 20),
    )(*operands)


def project_kernel(chunks, heads_ref, weight_ref, out_ref, held, sems):
    depth = weight_ref.shape[0] // chunks
    copies = []
    for i in range(chunks):
        rows = pl.ds(i * depth, depth)
        copies.append(pltpu.make_async_copy(weight_ref.at[rows], held.at[rows], sems.at[i]))
        copies[i].start()
    total = jnp.zeros(out_ref.shape, F32)
    for i in range(chunks):
        copies[i].wait()
        span = slice(i * depth, (i + 1) * depth)
        total = total + jnp.dot(heads_ref[:, span], held[span], preferred_element_type=F32)
    out_ref[...] = total.astype(BF)


def project(heads, weight):
    chunks = weight.shape[0] // LANES
    whole = pl.BlockSpec(memory_space=pltpu.VMEM)
    return pl.pallas_call(
        functools.partial(project_kernel, chunks),
        out_shape=pltpu.VMEM((heads.shape[0], weight.shape[1]), BF),
        in_specs=[whole, pl.BlockSpec(memory_space=pl.ANY)],
        out_specs=whole,
        scratch_shapes=[pltpu.VMEM(weight.shape, BF), pltpu.SemaphoreType.DMA((chunks,))],
        compiler_params=pltpu.CompilerParams(vmem_limit_bytes=14 << 20),
    )(heads, pltpu.with_memory_space_constraint(weight, pltpu.HBM))


def hidden_of(planes, rows_ref, gate_ref, up_ref):
    rows = rows_ref[...]
    gate_value = jnp.dot(rows, gate_ref[...], preferred_element_type=F32)
    up_value = jnp.dot(rows, up_ref[...], preferred_element_type=F32)
    hidden = jax.nn.silu(gate_value) * up_value
    x_count, tensor_count = planes
    cap = hidden.shape[0] // (x_count * tensor_count)
    order = [x * tensor_count + t for t in range(tensor_count) for x in range(x_count)]
    return jnp.concatenate([hidden[k * cap : (k + 1) * cap] for k in order], axis=0).astype(BF)


def own_kernel(planes, rows_ref, gate_ref, up_ref, out_ref):
    out_ref[...] = hidden_of(planes, rows_ref, gate_ref, up_ref)


def both_kernel(planes, own_ref, rows_ref, gate_ref, up_ref, out_ref):
    half = own_ref.shape[0]
    other = hidden_of(planes, rows_ref, gate_ref, up_ref)
    for peer in range(planes[0]):
        out_ref[peer, :half] = own_ref[...]
        out_ref[peer, half:] = other


def down_of(start, stop, source_ref, hidden_ref, down_refs):
    total = None
    for index, down_ref in enumerate(down_refs):
        part = jnp.dot(
            hidden_ref[source_ref[index], start:stop], down_ref[...], preferred_element_type=F32
        )
        total = part if total is None else total + part
    return total


def other_down_kernel(source_ref, hidden_ref, *refs):
    *down_refs, out_ref = refs
    rows = out_ref.shape[0]
    out_ref[...] = down_of(rows, 2 * rows, source_ref, hidden_ref, down_refs).astype(BF)


def own_down_kernel(source_ref, hidden_ref, arrived_ref, *refs):
    *down_refs, out_ref = refs
    rows = out_ref.shape[0]
    own = down_of(0, rows, source_ref, hidden_ref, down_refs)
    out_ref[...] = (own + arrived_ref[...].astype(F32)).astype(BF)


def on_device(attn_heads, out_proj, norm_gain, router, expert_ids, w_gate, w_up, w_down):
    tensor_count = lax.axis_size("tensor")
    x_count = lax.axis_size("x")
    expert_axes = ("y", "w")
    expert_count = lax.axis_size(expert_axes)
    swap = [(0, 1), (1, 0)]
    head_rows = attn_heads.reshape(-1, attn_heads.shape[-1])
    tok_rows = head_rows.shape[0] // tensor_count
    width = out_proj.shape[1]
    send_cap = max(2, tok_rows // (expert_count // 2))
    recv_cap = min(tok_rows + max(2, tok_rows // 5), send_cap * (expert_count - 2) + 2)
    slots = expert_count * send_cap

    pad_rows = -(-tok_rows // 8) * 8
    heads = head_rows.reshape(tensor_count, tok_rows, -1)
    heads = jnp.pad(heads, ((0, 0), (0, pad_rows - tok_rows), (0, 0)))
    partial = project(heads.reshape(tensor_count * pad_rows, -1), out_proj)
    partial = exchange(partial.reshape(tensor_count, pad_rows, width), "tensor")
    attended = total_of(partial)[:tok_rows]

    inverse = lax.rsqrt(jnp.mean(attended * attended, axis=-1, keepdims=True) + 1e-05)
    normed = attended * inverse * norm_gain
    router_logits = jnp.dot(normed.astype(BF), router, preferred_element_type=F32)
    chosen_ids = expert_ids.reshape(-1)
    expert_index = jnp.arange(expert_count, dtype=jnp.int32)
    member_mask = chosen_ids[:, None] == expert_index[None, :]
    router_score = jax.nn.sigmoid(jnp.sum(jnp.where(member_mask, router_logits, 0.0), axis=1))
    routed = (normed * router_score[:, None]).astype(BF)

    same = chosen_ids[:, None] == chosen_ids[None, :]
    earlier = jnp.arange(tok_rows)[None, :] < jnp.arange(tok_rows)[:, None]
    rank_within = jnp.sum((same & earlier).astype(jnp.int32), axis=1)
    slot_index = chosen_ids * send_cap + rank_within
    slot_range = jnp.arange(slots, dtype=jnp.int32)
    placing = (slot_range[:, None] == slot_index[None, :]).astype(BF)
    flagged = jnp.concatenate([routed, jnp.ones((tok_rows, LANES), BF)], axis=1)
    outgoing = jnp.dot(placing, flagged, preferred_element_type=F32).astype(BF)
    place = lax.axis_index("x")
    columns = width // x_count
    outgoing, down = lax.optimization_barrier((outgoing, w_down[0]))
    sources, downs = [place], [lax.dynamic_slice_in_dim(down, place * columns, columns, 1)]
    for step in range(1, x_count):
        to = (place + step) % x_count
        piece = lax.dynamic_slice_in_dim(down, to * columns, columns, 1)
        ring = [(i, (i + step) % x_count) for i in range(x_count)]
        sources.append((place + x_count - step) % x_count)
        downs.append(lax.ppermute(piece, "x", ring))
    sources = jnp.stack(sources).astype(jnp.int32)
    arrived = exchange(outgoing.reshape(expert_count, send_cap, width + LANES), expert_axes)
    arrived, downs = lax.optimization_barrier((arrived, downs))
    arrived = arrived.reshape(slots, width + LANES)

    filled = arrived[:, width].astype(F32)
    before = slot_range[:, None] < slot_range[None, :]
    position = jnp.sum(jnp.where(before, filled[:, None], 0.0), axis=0).astype(jnp.int32)
    position = jnp.where(filled > 0.5, position, -1)
    selector = (jnp.arange(recv_cap, dtype=jnp.int32)[:, None] == position[None, :]).astype(BF)
    compact = jnp.dot(selector, arrived[:, :width], preferred_element_type=F32).astype(BF)

    rows = spread(compact, "tensor").reshape(tensor_count * recv_cap, width)
    rows = spread(rows, "x").reshape(x_count * tensor_count * recv_cap, width)
    other_rows = lax.ppermute(rows, "core", swap)

    gate, up = w_gate[0], w_up[0]
    units = gate.shape[1]
    half = rows.shape[0]
    planes = (x_count, tensor_count)
    own_hidden = local_call(
        functools.partial(own_kernel, planes), (half, units), rows, gate, up
    )
    own_hidden, other_rows = lax.optimization_barrier((own_hidden, other_rows))
    hidden = local_call(
        functools.partial(both_kernel, planes),
        (x_count, 2 * half, units),
        own_hidden,
        other_rows,
        gate,
        up,
    )
    hidden = exchange(hidden, "x")
    other_sum = local_call(other_down_kernel, (half, columns), sources, hidden, *downs)
    other_sum = lax.ppermute(other_sum, "core", swap)
    pair_sum = local_call(
        own_down_kernel, (half, columns), sources, hidden, other_sum, *downs
    )
    column_sum = total_of(
        exchange(pair_sum.reshape(tensor_count, x_count * recv_cap, columns), "tensor")
    ).astype(BF)
    expert_rows = exchange(column_sum.reshape(x_count, recv_cap, columns), "x")
    expert_rows = expert_rows.transpose(1, 0, 2).reshape(recv_cap, width)

    back = jnp.dot(selector.T, expert_rows, preferred_element_type=F32).astype(BF)
    returned = exchange(back.reshape(expert_count, send_cap, width), expert_axes)
    combined = jnp.dot(placing.T, returned.reshape(slots, width), preferred_element_type=F32)
    return combined.astype(BF).reshape(1, tok_rows, 1, width)


def solution(mesh):
    dp, tensor, expert = (mesh.shape[name] for name in ("dp", "tensor", "expert"))
    fine = Mesh(
        mesh.devices.reshape(dp // 2, 2, tensor, expert // 3, 3), ("x", "core", "tensor", "y", "w")
    )
    dp_axes, expert_axes = ("x", "core"), ("y", "w")
    in_specs = (
        P(dp_axes, None, expert_axes, "tensor"),
        P("tensor", None),
        P(),
        P(),
        P(dp_axes, "tensor", expert_axes),
        P(expert_axes, None, (*dp_axes, "tensor")),
        P(expert_axes, None, (*dp_axes, "tensor")),
        P(expert_axes, (*dp_axes, "tensor"), None),
    )
    out_specs = P(dp_axes, "tensor", expert_axes, None)
    return jax.shard_map(
        on_device, mesh=fine, in_specs=in_specs, out_specs=out_specs, check_vma=False
    )
```

```python
import functools

import jax
import jax.numpy as jnp
from jax import lax
from jax.experimental import pallas as pl
from jax.experimental.pallas import tpu as pltpu
from jax.sharding import Mesh, PartitionSpec as P

BF = jnp.bfloat16
F32 = jnp.float32
LANES = 128


def exchange(value, axis):
    return lax.all_to_all(value, axis, split_axis=0, concat_axis=0, tiled=True)


def spread(value, axis):
    count = lax.axis_size(axis)
    return exchange(jnp.broadcast_to(value[None], (count,) + value.shape), axis)


def total_of(parts):
    total = parts[0].astype(F32)
    for index in range(1, parts.shape[0]):
        total = total + parts[index].astype(F32)
    return total


def in_vmem(value):
    return pltpu.with_memory_space_constraint(value, pltpu.VMEM)


def local_call(kernel, shape, *operands):
    whole = pl.BlockSpec(memory_space=pltpu.VMEM)
    return pl.pallas_call(
        kernel,
        out_shape=pltpu.VMEM(shape, BF),
        in_specs=[whole] * len(operands),
        out_specs=whole,
        compiler_params=pltpu.CompilerParams(vmem_limit_bytes=14 << 20),
    )(*operands)


def project_kernel(chunks, heads_ref, weight_ref, out_ref, held, sems):
    depth = weight_ref.shape[0] // chunks
    copies = []
    for i in range(chunks):
        rows = pl.ds(i * depth, depth)
        copies.append(pltpu.make_async_copy(weight_ref.at[rows], held.at[rows], sems.at[i]))
        copies[i].start()
    total = jnp.zeros(out_ref.shape, F32)
    for i in range(chunks):
        copies[i].wait()
        span = slice(i * depth, (i + 1) * depth)
        total = total + jnp.dot(heads_ref[:, span], held[span], preferred_element_type=F32)
    out_ref[...] = total.astype(BF)


def project(heads, weight):
    chunks = weight.shape[0] // LANES
    whole = pl.BlockSpec(memory_space=pltpu.VMEM)
    return pl.pallas_call(
        functools.partial(project_kernel, chunks),
        out_shape=pltpu.VMEM((heads.shape[0], weight.shape[1]), BF),
        in_specs=[whole, pl.BlockSpec(memory_space=pl.ANY)],
        out_specs=whole,
        scratch_shapes=[pltpu.VMEM(weight.shape, BF), pltpu.SemaphoreType.DMA((chunks,))],
        compiler_params=pltpu.CompilerParams(vmem_limit_bytes=14 << 20),
    )(heads, pltpu.with_memory_space_constraint(weight, pltpu.HBM))


def expert_kernel(rows_ref, *refs):
    *weight_refs, out_ref = refs
    rows = rows_ref[...]
    hiddens = []
    for gate_ref, up_ref in (weight_refs[0:2], weight_refs[3:5]):
        gate_value = jnp.dot(rows, gate_ref[...], preferred_element_type=F32)
        up_value = jnp.dot(rows, up_ref[...], preferred_element_type=F32)
        hiddens.append((jax.nn.silu(gate_value) * up_value).astype(BF))
    block = 1280
    for start in range(0, out_ref.shape[1], block):
        span = slice(start, start + block)
        total = jnp.dot(hiddens[0], weight_refs[2][:, span], preferred_element_type=F32)
        total = total + jnp.dot(hiddens[1], weight_refs[5][:, span], preferred_element_type=F32)
        out_ref[:, span] = total.astype(BF)


def on_device(attn_heads, out_proj, norm_gain, router, expert_ids, w_gate, w_up, w_down):
    tensor_count = lax.axis_size("tensor")
    x_count = lax.axis_size("x")
    expert_axes = ("y", "w")
    expert_count = lax.axis_size(expert_axes)
    swap = [(0, 1), (1, 0)]
    head_rows = attn_heads.reshape(-1, attn_heads.shape[-1])
    tok_rows = head_rows.shape[0] // tensor_count
    width = out_proj.shape[1]
    send_cap = max(2, tok_rows // (expert_count // 2))
    recv_cap = min(tok_rows + max(2, tok_rows // 5), send_cap * (expert_count - 2) + 2)
    slots = expert_count * send_cap

    pad_rows = -(-tok_rows // 8) * 8
    heads = head_rows.reshape(tensor_count, tok_rows, -1)
    heads = jnp.pad(heads, ((0, 0), (0, pad_rows - tok_rows), (0, 0)))
    partial = project(heads.reshape(tensor_count * pad_rows, -1), out_proj)
    partial = exchange(partial.reshape(tensor_count, pad_rows, width), "tensor")
    attended = total_of(partial)[:tok_rows]

    inverse = lax.rsqrt(jnp.mean(attended * attended, axis=-1, keepdims=True) + 1e-05)
    normed = attended * inverse * norm_gain
    router_logits = jnp.dot(normed.astype(BF), router, preferred_element_type=F32)
    chosen_ids = expert_ids.reshape(-1)
    expert_index = jnp.arange(expert_count, dtype=jnp.int32)
    member_mask = chosen_ids[:, None] == expert_index[None, :]
    router_score = jax.nn.sigmoid(jnp.sum(jnp.where(member_mask, router_logits, 0.0), axis=1))
    routed = (normed * router_score[:, None]).astype(BF)

    same = chosen_ids[:, None] == chosen_ids[None, :]
    earlier = jnp.arange(tok_rows)[None, :] < jnp.arange(tok_rows)[:, None]
    rank_within = jnp.sum((same & earlier).astype(jnp.int32), axis=1)
    slot_index = chosen_ids * send_cap + rank_within
    slot_range = jnp.arange(slots, dtype=jnp.int32)
    placing = (slot_range[:, None] == slot_index[None, :]).astype(BF)
    flagged = jnp.concatenate([routed, jnp.ones((tok_rows, LANES), BF)], axis=1)
    outgoing = jnp.dot(placing, flagged, preferred_element_type=F32).astype(BF)
    own = [weight[0] for weight in (w_gate, w_up, w_down)]
    outgoing, own = lax.optimization_barrier((outgoing, own))
    other = [lax.ppermute(weight, "core", swap) for weight in own]
    arrived = exchange(outgoing.reshape(expert_count, send_cap, width + LANES), expert_axes)
    arrived, other = lax.optimization_barrier((arrived, other))
    arrived = arrived.reshape(slots, width + LANES)

    filled = arrived[:, width].astype(F32)
    before = slot_range[:, None] < slot_range[None, :]
    position = jnp.sum(jnp.where(before, filled[:, None], 0.0), axis=0).astype(jnp.int32)
    position = jnp.where(filled > 0.5, position, -1)
    selector = (jnp.arange(recv_cap, dtype=jnp.int32)[:, None] == position[None, :]).astype(BF)
    compact = jnp.dot(selector, arrived[:, :width], preferred_element_type=F32).astype(BF)

    rows = spread(compact, "tensor").reshape(tensor_count * recv_cap, width)
    rows = spread(rows, "x").reshape(x_count * tensor_count * recv_cap, width)
    pair_sum = local_call(expert_kernel, rows.shape, rows, *own, *other)
    plane_sum = total_of(
        exchange(pair_sum.reshape(x_count, tensor_count * recv_cap, width), "x")
    ).astype(BF)
    expert_rows = total_of(
        exchange(plane_sum.reshape(tensor_count, recv_cap, width), "tensor")
    ).astype(BF)

    back = jnp.dot(selector.T, expert_rows, preferred_element_type=F32).astype(BF)
    returned = exchange(back.reshape(expert_count, send_cap, width), expert_axes)
    combined = jnp.dot(placing.T, returned.reshape(slots, width), preferred_element_type=F32)
    return combined.astype(BF).reshape(1, tok_rows, 1, width)


def solution(mesh):
    dp, tensor, expert = (mesh.shape[name] for name in ("dp", "tensor", "expert"))
    fine = Mesh(
        mesh.devices.reshape(dp // 2, 2, tensor, expert // 3, 3), ("x", "core", "tensor", "y", "w")
    )
    dp_axes, expert_axes = ("x", "core"), ("y", "w")
    in_specs = (
        P(dp_axes, None, expert_axes, "tensor"),
        P("tensor", None),
        P(),
        P(),
        P(dp_axes, "tensor", expert_axes),
        P(expert_axes, None, (*dp_axes, "tensor")),
        P(expert_axes, None, (*dp_axes, "tensor")),
        P(expert_axes, (*dp_axes, "tensor"), None),
    )
    out_specs = P(dp_axes, "tensor", expert_axes, None)
    return jax.shard_map(
        on_device, mesh=fine, in_specs=in_specs, out_specs=out_specs, check_vma=False
    )
```

```python
import functools

import jax
import jax.numpy as jnp
from jax import lax
from jax.experimental import pallas as pl
from jax.experimental.pallas import tpu as pltpu
from jax.sharding import Mesh, PartitionSpec as P

BF = jnp.bfloat16
F32 = jnp.float32
LANES = 128


def exchange(value, axis):
    return lax.all_to_all(value, axis, split_axis=0, concat_axis=0, tiled=True)


def spread(value, axis):
    count = lax.axis_size(axis)
    return exchange(jnp.broadcast_to(value[None], (count,) + value.shape), axis)


def total_of(parts):
    total = parts[0].astype(F32)
    for index in range(1, parts.shape[0]):
        total = total + parts[index].astype(F32)
    return total


def in_vmem(value):
    return pltpu.with_memory_space_constraint(value, pltpu.VMEM)


def local_call(kernel, shape, *operands):
    whole = pl.BlockSpec(memory_space=pltpu.VMEM)
    return pl.pallas_call(
        kernel,
        out_shape=pltpu.VMEM(shape, BF),
        in_specs=[whole] * len(operands),
        out_specs=whole,
        compiler_params=pltpu.CompilerParams(vmem_limit_bytes=14 << 20),
    )(*operands)


def folds(tok_rows, width):
    wide = tok_rows * width // 8
    rest = width - wide
    each = wide // rest
    return wide, [(k, tok_rows + k // each, k % each * rest) for k in range(tok_rows)]


def project_kernel(chunks, tok_rows, heads_ref, weight_ref, out_ref, held, packed, sems):
    depth = weight_ref.shape[0] // chunks
    width = weight_ref.shape[1]
    copies = []
    for i in range(chunks):
        rows = pl.ds(i * depth, depth)
        copies.append(pltpu.make_async_copy(weight_ref.at[rows], held.at[rows], sems.at[i]))
        copies[i].start()
    total = jnp.zeros((heads_ref.shape[0], width), F32)
    for i in range(chunks):
        copies[i].wait()
        span = slice(i * depth, (i + 1) * depth)
        total = total + jnp.dot(heads_ref[:, span], held[span], preferred_element_type=F32)
    wide, places = folds(tok_rows, width)
    for peer in range(heads_ref.shape[0] // tok_rows):
        token = peer * tok_rows
        packed[8 * peer : 8 * peer + tok_rows] = total[token : token + tok_rows, :wide]
        for k, row, column in places:
            packed[8 * peer + row : 8 * peer + row + 1, column : column + width - wide] = total[
                token + k : token + k + 1, wide:
            ]
    out_ref[...] = packed[...].astype(BF)


def project(heads, weight, tok_rows):
    chunks = weight.shape[0] // LANES
    wide, _ = folds(tok_rows, weight.shape[1])
    packed_shape = (heads.shape[0] // tok_rows * 8, wide)
    whole = pl.BlockSpec(memory_space=pltpu.VMEM)
    return pl.pallas_call(
        functools.partial(project_kernel, chunks, tok_rows),
        out_shape=pltpu.VMEM(packed_shape, BF),
        in_specs=[whole, pl.BlockSpec(memory_space=pl.ANY)],
        out_specs=whole,
        scratch_shapes=[
            pltpu.VMEM(weight.shape, BF),
            pltpu.VMEM(packed_shape, F32),
            pltpu.SemaphoreType.DMA((chunks,)),
        ],
        compiler_params=pltpu.CompilerParams(vmem_limit_bytes=14 << 20),
    )(heads, pltpu.with_memory_space_constraint(weight, pltpu.HBM))


def route_kernel(
    tok_rows, parts_ref, gain_ref, router_ref, member_ref, placing_ref, out_ref, attended_ref
):
    width = gain_ref.shape[1]
    packed = parts_ref[0].astype(F32)
    for index in range(1, parts_ref.shape[0]):
        packed = packed + parts_ref[index].astype(F32)
    wide, places = folds(tok_rows, width)
    attended_ref[...] = jnp.zeros(attended_ref.shape, F32)
    attended_ref[:tok_rows, :wide] = packed[:tok_rows]
    for k, row, column in places:
        attended_ref[k : k + 1, wide:] = packed[row : row + 1, column : column + width - wide]
    attended = attended_ref[...]
    inverse = lax.rsqrt(jnp.mean(attended * attended, axis=1, keepdims=True) + 1e-05)
    normed = attended * inverse * gain_ref[...]
    logits = lax.dot_general(
        normed.astype(BF),
        router_ref[...],
        (((1,), (1,)), ((), ())),
        preferred_element_type=F32,
    )
    picked = jnp.sum(jnp.where(member_ref[...] > 0, logits, 0.0), axis=1, keepdims=True)
    routed = (normed * jax.nn.sigmoid(picked)).astype(BF)
    placing = placing_ref[...]
    out_ref[:, :width] = jnp.dot(placing, routed, preferred_element_type=F32).astype(BF)
    filled = jnp.sum(placing.astype(F32), axis=1, keepdims=True)
    out_ref[:, width:] = jnp.broadcast_to(filled, (placing.shape[0], LANES)).astype(BF)


def route(parts, gain, router_rows, member, placing, tok_rows):
    whole = pl.BlockSpec(memory_space=pltpu.VMEM)
    width = gain.shape[1]
    return pl.pallas_call(
        functools.partial(route_kernel, tok_rows),
        out_shape=jax.ShapeDtypeStruct((placing.shape[0], width + LANES), BF),
        in_specs=[whole] * 5,
        out_specs=whole,
        scratch_shapes=[pltpu.VMEM((8, width), F32)],
        compiler_params=pltpu.CompilerParams(vmem_limit_bytes=8 << 20),
    )(parts, gain, router_rows, member, placing)


def expert_kernel(rows_ref, *refs):
    *weight_refs, out_ref = refs
    rows = rows_ref[...]
    hiddens = []
    for gate_ref, up_ref in (weight_refs[0:2], weight_refs[3:5]):
        gate_value = jnp.dot(rows, gate_ref[...], preferred_element_type=F32)
        up_value = jnp.dot(rows, up_ref[...], preferred_element_type=F32)
        hiddens.append((jax.nn.silu(gate_value) * up_value).astype(BF))
    block = 1280
    for start in range(0, out_ref.shape[1], block):
        span = slice(start, start + block)
        total = jnp.dot(hiddens[0], weight_refs[2][:, span], preferred_element_type=F32)
        total = total + jnp.dot(hiddens[1], weight_refs[5][:, span], preferred_element_type=F32)
        out_ref[:, span] = total.astype(BF)


def on_device(attn_heads, out_proj, norm_gain, router, expert_ids, w_gate, w_up, w_down):
    tensor_count = lax.axis_size("tensor")
    x_count = lax.axis_size("x")
    expert_axes = ("y", "w")
    expert_count = lax.axis_size(expert_axes)
    swap = [(0, 1), (1, 0)]
    head_rows = attn_heads.reshape(-1, attn_heads.shape[-1])
    tok_rows = head_rows.shape[0] // tensor_count
    width = out_proj.shape[1]
    send_cap = max(2, tok_rows // (expert_count // 2))
    recv_cap = min(tok_rows + max(2, tok_rows // 5), send_cap * (expert_count - 2) + 2)
    slots = expert_count * send_cap

    chosen_ids = expert_ids.reshape(-1)
    expert_index = jnp.arange(expert_count, dtype=jnp.int32)
    member = (chosen_ids[:, None] == expert_index[None, :]).astype(F32)
    same = chosen_ids[:, None] == chosen_ids[None, :]
    earlier = jnp.arange(tok_rows)[None, :] < jnp.arange(tok_rows)[:, None]
    rank_within = jnp.sum((same & earlier).astype(jnp.int32), axis=1)
    slot_index = chosen_ids * send_cap + rank_within
    slot_range = jnp.arange(slots, dtype=jnp.int32)
    placing = (slot_range[:, None] == slot_index[None, :]).astype(BF)
    spare = 8 - tok_rows

    gate, up, down = w_gate[0], w_up[0], w_down[0]
    partial = project(head_rows, out_proj, tok_rows)
    parts = exchange(partial.reshape(tensor_count, 8, -1), "tensor")
    outgoing = route(
        parts,
        norm_gain[None],
        router.T,
        jnp.pad(member, ((0, spare), (0, 0))),
        jnp.pad(placing, ((0, 0), (0, spare))),
        tok_rows,
    )
    outgoing, gate, up = lax.optimization_barrier((outgoing, gate, up))
    other_gate = lax.ppermute(gate, "core", swap)
    other_up = lax.ppermute(up, "core", swap)
    arrived = exchange(outgoing.reshape(expert_count, send_cap, width + LANES), expert_axes)
    arrived, other_gate, other_up = lax.optimization_barrier((arrived, other_gate, other_up))
    arrived = arrived.reshape(slots, width + LANES)

    filled = arrived[:, width].astype(F32)
    before = slot_range[:, None] < slot_range[None, :]
    position = jnp.sum(jnp.where(before, filled[:, None], 0.0), axis=0).astype(jnp.int32)
    position = jnp.where(filled > 0.5, position, -1)
    selector = (jnp.arange(recv_cap, dtype=jnp.int32)[:, None] == position[None, :]).astype(BF)
    compact = jnp.dot(selector, arrived[:, :width], preferred_element_type=F32).astype(BF)

    compact, down = lax.optimization_barrier((compact, down))
    other_down = lax.ppermute(down, "core", swap)
    rows = spread(compact, "tensor").reshape(tensor_count * recv_cap, width)
    rows, other_down = lax.optimization_barrier((rows, other_down))
    rows = spread(rows, "x").reshape(x_count * tensor_count * recv_cap, width)
    pair_sum = local_call(
        expert_kernel, rows.shape, rows, gate, up, down, other_gate, other_up, other_down
    )
    plane_sum = total_of(
        exchange(pair_sum.reshape(x_count, tensor_count * recv_cap, width), "x")
    ).astype(BF)
    expert_rows = total_of(
        exchange(plane_sum.reshape(tensor_count, recv_cap, width), "tensor")
    ).astype(BF)

    back = jnp.dot(selector.T, expert_rows, preferred_element_type=F32).astype(BF)
    returned = exchange(back.reshape(expert_count, send_cap, width), expert_axes)
    combined = jnp.dot(placing.T, returned.reshape(slots, width), preferred_element_type=F32)
    return combined.astype(BF).reshape(1, tok_rows, 1, width)


def solution(mesh):
    dp, tensor, expert = (mesh.shape[name] for name in ("dp", "tensor", "expert"))
    fine = Mesh(
        mesh.devices.reshape(dp // 2, 2, tensor, expert // 3, 3), ("x", "core", "tensor", "y", "w")
    )
    dp_axes, expert_axes = ("x", "core"), ("y", "w")
    in_specs = (
        P(dp_axes, None, expert_axes, "tensor"),
        P("tensor", None),
        P(),
        P(),
        P(dp_axes, "tensor", expert_axes),
        P(expert_axes, None, (*dp_axes, "tensor")),
        P(expert_axes, None, (*dp_axes, "tensor")),
        P(expert_axes, (*dp_axes, "tensor"), None),
    )
    out_specs = P(dp_axes, "tensor", expert_axes, None)
    return jax.shard_map(
        on_device, mesh=fine, in_specs=in_specs, out_specs=out_specs, check_vma=False
    )
```

```python
import functools

import jax
import jax.numpy as jnp
from jax import lax
from jax.experimental import pallas as pl
from jax.experimental.pallas import tpu as pltpu
from jax.sharding import Mesh, PartitionSpec as P

BF = jnp.bfloat16
F32 = jnp.float32
LANES = 128


def exchange(value, axis):
    return lax.all_to_all(value, axis, split_axis=0, concat_axis=0, tiled=True)


def spread(value, axis):
    count = lax.axis_size(axis)
    return exchange(jnp.broadcast_to(value[None], (count,) + value.shape), axis)


def total_of(parts):
    total = parts[0].astype(F32)
    for index in range(1, parts.shape[0]):
        total = total + parts[index].astype(F32)
    return total


def in_vmem(value):
    return pltpu.with_memory_space_constraint(value, pltpu.VMEM)


def local_call(kernel, shape, *operands):
    whole = pl.BlockSpec(memory_space=pltpu.VMEM)
    return pl.pallas_call(
        kernel,
        out_shape=pltpu.VMEM(shape, BF),
        in_specs=[whole] * len(operands),
        out_specs=whole,
        compiler_params=pltpu.CompilerParams(vmem_limit_bytes=14 << 20),
    )(*operands)


def folds(tok_rows, width):
    wide = tok_rows * width // 8
    rest = width - wide
    each = wide // rest
    return wide, [(k, tok_rows + k // each, k % each * rest) for k in range(tok_rows)]


def project_kernel(chunks, tok_rows, heads_ref, weight_ref, out_ref, held, packed, sems):
    depth = weight_ref.shape[0] // chunks
    width = weight_ref.shape[1]
    copies = []
    for i in range(chunks):
        rows = pl.ds(i * depth, depth)
        copies.append(pltpu.make_async_copy(weight_ref.at[rows], held.at[rows], sems.at[i]))
        copies[i].start()
    total = jnp.zeros((heads_ref.shape[0], width), F32)
    for i in range(chunks):
        copies[i].wait()
        span = slice(i * depth, (i + 1) * depth)
        total = total + jnp.dot(heads_ref[:, span], held[span], preferred_element_type=F32)
    wide, places = folds(tok_rows, width)
    for peer in range(heads_ref.shape[0] // tok_rows):
        token = peer * tok_rows
        packed[8 * peer : 8 * peer + tok_rows] = total[token : token + tok_rows, :wide]
        for k, row, column in places:
            packed[8 * peer + row : 8 * peer + row + 1, column : column + width - wide] = total[
                token + k : token + k + 1, wide:
            ]
    out_ref[...] = packed[...].astype(BF)


def project(heads, weight, tok_rows):
    chunks = weight.shape[0] // LANES
    wide, _ = folds(tok_rows, weight.shape[1])
    packed_shape = (heads.shape[0] // tok_rows * 8, wide)
    whole = pl.BlockSpec(memory_space=pltpu.VMEM)
    return pl.pallas_call(
        functools.partial(project_kernel, chunks, tok_rows),
        out_shape=pltpu.VMEM(packed_shape, BF),
        in_specs=[whole, pl.BlockSpec(memory_space=pl.ANY)],
        out_specs=whole,
        scratch_shapes=[
            pltpu.VMEM(weight.shape, BF),
            pltpu.VMEM(packed_shape, F32),
            pltpu.SemaphoreType.DMA((chunks,)),
        ],
        compiler_params=pltpu.CompilerParams(vmem_limit_bytes=14 << 20),
    )(heads, pltpu.with_memory_space_constraint(weight, pltpu.HBM))


def stacked(rows, fold):
    part = rows.shape[1] // fold
    return jnp.concatenate([rows[:, q * part : (q + 1) * part] for q in range(fold)], axis=0)


def turned(left, right):
    return lax.dot_general(left, right, (((0,), (0,)), ((), ())), preferred_element_type=F32)


def sum_of(parts_ref):
    total = parts_ref[0].astype(F32)
    for index in range(1, parts_ref.shape[0]):
        total = total + parts_ref[index].astype(F32)
    return total


def route_kernel(
    tok_rows, fold, parts_ref, gain_ref, router_ref, member_ref, placing_ref, out_ref, attended_ref
):
    width = gain_ref.shape[1]
    packed = sum_of(parts_ref)
    wide, places = folds(tok_rows, width)
    attended_ref[...] = jnp.zeros(attended_ref.shape, F32)
    attended_ref[:tok_rows, :wide] = packed[:tok_rows]
    for k, row, column in places:
        attended_ref[k : k + 1, wide:] = packed[row : row + 1, column : column + width - wide]
    attended = attended_ref[...]
    inverse = lax.rsqrt(jnp.mean(attended * attended, axis=1, keepdims=True) + 1e-05)
    normed = attended * inverse * gain_ref[...]
    logits = lax.dot_general(
        normed.astype(BF),
        router_ref[...],
        (((1,), (1,)), ((), ())),
        preferred_element_type=F32,
    )
    picked = jnp.sum(jnp.where(member_ref[...] > 0, logits, 0.0), axis=1, keepdims=True)
    routed = stacked(normed * jax.nn.sigmoid(picked), fold).astype(BF)
    out_ref[...] = jnp.dot(placing_ref[...], routed, preferred_element_type=F32).astype(BF)


def route(parts, gain, router_rows, member, placing, tok_rows, fold):
    whole = pl.BlockSpec(memory_space=pltpu.VMEM)
    width = gain.shape[1]
    return pl.pallas_call(
        functools.partial(route_kernel, tok_rows, fold),
        out_shape=jax.ShapeDtypeStruct((placing.shape[0], width // fold), BF),
        in_specs=[whole] * 5,
        out_specs=whole,
        scratch_shapes=[pltpu.VMEM((8, width), F32)],
        compiler_params=pltpu.CompilerParams(vmem_limit_bytes=8 << 20),
    )(parts, gain, router_rows, member, placing)


def compact_kernel(fold, cap, arrived_ref, out_ref, selector_ref):
    arrived = arrived_ref[...]
    rows = arrived.shape[0]
    square = (rows, rows)
    first = lax.broadcasted_iota(jnp.int32, square, 0)
    second = lax.broadcasted_iota(jnp.int32, square, 1)
    slot_first = lax.div(first, jnp.full(square, fold, jnp.int32))
    slot_second = lax.div(second, jnp.full(square, fold, jnp.int32))
    peak = jnp.max(jnp.abs(arrived.astype(F32)), axis=1, keepdims=True)
    filled = jnp.broadcast_to(jnp.where(peak > 0, 1.0, 0.0), (rows, LANES)).astype(BF)
    same = jnp.where(slot_first == slot_second, 1.0, 0.0).astype(BF)
    filled = jnp.dot(same, filled, preferred_element_type=F32) > 0
    heads = slot_second * fold == second
    before = jnp.where(heads & (slot_second < slot_first), 1.0, 0.0).astype(BF)
    ones = jnp.where(filled, 1.0, 0.0).astype(BF)
    position = jnp.dot(before, ones, preferred_element_type=F32).astype(jnp.int32)
    wide = (rows, LANES)
    row = lax.broadcasted_iota(jnp.int32, wide, 0)
    column = lax.broadcasted_iota(jnp.int32, wide, 1)
    piece = lax.div(column, jnp.full(wide, cap, jnp.int32))
    mine = lax.rem(row, jnp.full(wide, fold, jnp.int32)) == piece
    taken = filled & mine & (position == column - piece * cap)
    selector = jnp.where(taken, 1.0, 0.0).astype(BF)[:, : fold * cap]
    selector_ref[...] = selector
    compact = turned(selector, arrived)
    part = arrived.shape[1]
    for peer in range(out_ref.shape[0]):
        for q in range(fold):
            out_ref[peer, :, q * part : (q + 1) * part] = compact[
                q * cap : (q + 1) * cap
            ].astype(BF)


def compact_rows(arrived, fold, cap, peers):
    whole = pl.BlockSpec(memory_space=pltpu.VMEM)
    rows, part = arrived.shape
    return pl.pallas_call(
        functools.partial(compact_kernel, fold, cap),
        out_shape=(
            pltpu.VMEM((peers, cap, fold * part), BF),
            jax.ShapeDtypeStruct((rows, fold * cap), BF),
        ),
        in_specs=[whole],
        out_specs=(whole, whole),
        compiler_params=pltpu.CompilerParams(vmem_limit_bytes=8 << 20),
    )(arrived)


def return_kernel(fold, parts_ref, selector_ref, out_ref):
    expert_rows = stacked(sum_of(parts_ref), fold).astype(BF)
    out_ref[...] = jnp.dot(selector_ref[...], expert_rows, preferred_element_type=F32).astype(BF)


def combine_kernel(tok_rows, fold, returned_ref, placing_ref, out_ref):
    combined = turned(placing_ref[...], returned_ref[...])
    part = returned_ref.shape[1]
    rows = combined.shape[0] // fold
    for q in range(fold):
        out_ref[:, q * part : (q + 1) * part] = combined[q * rows : q * rows + tok_rows].astype(BF)


def combine(returned, placing, tok_rows, fold):
    whole = pl.BlockSpec(memory_space=pltpu.VMEM)
    return pl.pallas_call(
        functools.partial(combine_kernel, tok_rows, fold),
        out_shape=jax.ShapeDtypeStruct((tok_rows, fold * returned.shape[1]), BF),
        in_specs=[whole] * 2,
        out_specs=whole,
        compiler_params=pltpu.CompilerParams(vmem_limit_bytes=8 << 20),
    )(returned, placing)


def expert_kernel(rows_ref, *refs):
    *weight_refs, out_ref = refs
    rows = rows_ref[...]
    hiddens = []
    for gate_ref, up_ref in (weight_refs[0:2], weight_refs[3:5]):
        gate_value = jnp.dot(rows, gate_ref[...], preferred_element_type=F32)
        up_value = jnp.dot(rows, up_ref[...], preferred_element_type=F32)
        hiddens.append((jax.nn.silu(gate_value) * up_value).astype(BF))
    block = 1280
    for start in range(0, out_ref.shape[1], block):
        span = slice(start, start + block)
        total = jnp.dot(hiddens[0], weight_refs[2][:, span], preferred_element_type=F32)
        total = total + jnp.dot(hiddens[1], weight_refs[5][:, span], preferred_element_type=F32)
        out_ref[:, span] = total.astype(BF)


def on_device(attn_heads, out_proj, norm_gain, router, expert_ids, w_gate, w_up, w_down):
    tensor_count = lax.axis_size("tensor")
    x_count = lax.axis_size("x")
    expert_axes = ("y", "w")
    expert_count = lax.axis_size(expert_axes)
    swap = [(0, 1), (1, 0)]
    head_rows = attn_heads.reshape(-1, attn_heads.shape[-1])
    tok_rows = head_rows.shape[0] // tensor_count
    width = out_proj.shape[1]
    send_cap = max(2, tok_rows // (expert_count // 2))
    recv_cap = min(tok_rows + max(2, tok_rows // 5), send_cap * (expert_count - 2) + 2)
    slots = expert_count * send_cap

    chosen_ids = expert_ids.reshape(-1)
    expert_index = jnp.arange(expert_count, dtype=jnp.int32)
    member = (chosen_ids[:, None] == expert_index[None, :]).astype(F32)
    same = chosen_ids[:, None] == chosen_ids[None, :]
    earlier = jnp.arange(tok_rows)[None, :] < jnp.arange(tok_rows)[:, None]
    rank_within = jnp.sum((same & earlier).astype(jnp.int32), axis=1)
    slot_index = chosen_ids * send_cap + rank_within
    spare = 8 - tok_rows
    fold = 8 // send_cap
    row_range = jnp.arange(slots * fold, dtype=jnp.int32)
    slot_columns = jnp.tile(jnp.pad(slot_index, (0, spare), constant_values=-1), fold)
    piece_columns = jnp.arange(fold * 8, dtype=jnp.int32) // 8
    target = jnp.where(slot_columns < 0, -1, slot_columns * fold + piece_columns)
    placing = (row_range[:, None] == target[None, :]).astype(BF)

    gate, up, down = w_gate[0], w_up[0], w_down[0]
    partial = project(head_rows, out_proj, tok_rows)
    parts = exchange(partial.reshape(tensor_count, 8, -1), "tensor")
    outgoing = route(
        parts,
        norm_gain[None],
        router.T,
        jnp.pad(member, ((0, spare), (0, 0))),
        placing,
        tok_rows,
        fold,
    )
    outgoing, gate, up = lax.optimization_barrier((outgoing, gate, up))
    other_gate = lax.ppermute(gate, "core", swap)
    other_up = lax.ppermute(up, "core", swap)
    arrived = exchange(outgoing, expert_axes)
    arrived, other_gate, other_up = lax.optimization_barrier((arrived, other_gate, other_up))
    compact, selector = compact_rows(arrived, fold, recv_cap, tensor_count)
    compact, down = lax.optimization_barrier((compact, down))
    other_down = lax.ppermute(down, "core", swap)
    rows = exchange(compact, "tensor").reshape(tensor_count * recv_cap, width)
    rows, other_down = lax.optimization_barrier((rows, other_down))
    rows = spread(rows, "x").reshape(x_count * tensor_count * recv_cap, width)
    pair_sum = local_call(
        expert_kernel, rows.shape, rows, gate, up, down, other_gate, other_up, other_down
    )
    plane_sum = total_of(
        exchange(pair_sum.reshape(x_count, tensor_count * recv_cap, width), "x")
    ).astype(BF)
    parts = exchange(plane_sum.reshape(tensor_count, recv_cap, width), "tensor")
    back = local_call(
        functools.partial(return_kernel, fold),
        (slots * fold, width // fold),
        parts,
        selector,
    )
    returned = exchange(back, expert_axes)
    combined = combine(returned, placing, tok_rows, fold)
    return combined.reshape(1, tok_rows, 1, width)


def solution(mesh):
    dp, tensor, expert = (mesh.shape[name] for name in ("dp", "tensor", "expert"))
    fine = Mesh(
        mesh.devices.reshape(dp // 2, 2, tensor, expert // 3, 3), ("x", "core", "tensor", "y", "w")
    )
    dp_axes, expert_axes = ("x", "core"), ("y", "w")
    in_specs = (
        P(dp_axes, None, expert_axes, "tensor"),
        P("tensor", None),
        P(),
        P(),
        P(dp_axes, "tensor", expert_axes),
        P(expert_axes, None, (*dp_axes, "tensor")),
        P(expert_axes, None, (*dp_axes, "tensor")),
        P(expert_axes, (*dp_axes, "tensor"), None),
    )
    out_specs = P(dp_axes, "tensor", expert_axes, None)
    return jax.shard_map(
        on_device, mesh=fine, in_specs=in_specs, out_specs=out_specs, check_vma=False
    )
```

```python
import functools

import jax
import jax.numpy as jnp
from jax import lax
from jax.experimental import pallas as pl
from jax.experimental.pallas import tpu as pltpu
from jax.sharding import Mesh, PartitionSpec as P

BF = jnp.bfloat16
F32 = jnp.float32
LANES = 128


def exchange(value, axis):
    return lax.all_to_all(value, axis, split_axis=0, concat_axis=0, tiled=True)


def spread(value, axis):
    count = lax.axis_size(axis)
    return exchange(jnp.broadcast_to(value[None], (count,) + value.shape), axis)


def total_of(parts):
    total = parts[0].astype(F32)
    for index in range(1, parts.shape[0]):
        total = total + parts[index].astype(F32)
    return total


def in_vmem(value):
    return pltpu.with_memory_space_constraint(value, pltpu.VMEM)


def local_call(kernel, shape, *operands):
    whole = pl.BlockSpec(memory_space=pltpu.VMEM)
    return pl.pallas_call(
        kernel,
        out_shape=pltpu.VMEM(shape, BF),
        in_specs=[whole] * len(operands),
        out_specs=whole,
        compiler_params=pltpu.CompilerParams(vmem_limit_bytes=14 << 20),
    )(*operands)


def folds(tok_rows, width):
    wide = tok_rows * width // 8
    rest = width - wide
    each = wide // rest
    return wide, [(k, tok_rows + k // each, k % each * rest) for k in range(tok_rows)]


def project_kernel(chunks, tok_rows, source_ref, weight_ref, out_ref, heads_ref, held, packed, sems):
    depth = weight_ref.shape[0] // chunks
    width = weight_ref.shape[1]
    fetch = pltpu.make_async_copy(source_ref, heads_ref, sems.at[chunks])
    fetch.start()
    copies = []
    for i in range(chunks):
        rows = pl.ds(i * depth, depth)
        copies.append(pltpu.make_async_copy(weight_ref.at[rows], held.at[rows], sems.at[i]))
        copies[i].start()
    fetch.wait()
    total = jnp.zeros((heads_ref.shape[0], width), F32)
    for i in range(chunks):
        copies[i].wait()
        span = slice(i * depth, (i + 1) * depth)
        total = total + jnp.dot(heads_ref[:, span], held[span], preferred_element_type=F32)
    wide, places = folds(tok_rows, width)
    for peer in range(heads_ref.shape[0] // tok_rows):
        token = peer * tok_rows
        packed[8 * peer : 8 * peer + tok_rows] = total[token : token + tok_rows, :wide]
        for k, row, column in places:
            packed[8 * peer + row : 8 * peer + row + 1, column : column + width - wide] = total[
                token + k : token + k + 1, wide:
            ]
    out_ref[...] = packed[...].astype(BF)


def project(heads, weight, tok_rows):
    chunks = weight.shape[0] // LANES
    wide, _ = folds(tok_rows, weight.shape[1])
    packed_shape = (heads.shape[0] // tok_rows * 8, wide)
    whole = pl.BlockSpec(memory_space=pltpu.VMEM)
    return pl.pallas_call(
        functools.partial(project_kernel, chunks, tok_rows),
        out_shape=pltpu.VMEM(packed_shape, BF),
        in_specs=[pl.BlockSpec(memory_space=pl.ANY)] * 2,
        out_specs=whole,
        scratch_shapes=[
            pltpu.VMEM(heads.shape, BF),
            pltpu.VMEM(weight.shape, BF),
            pltpu.VMEM(packed_shape, F32),
            pltpu.SemaphoreType.DMA((chunks + 1,)),
        ],
        compiler_params=pltpu.CompilerParams(vmem_limit_bytes=14 << 20),
    )(*[pltpu.with_memory_space_constraint(operand, pltpu.HBM) for operand in (heads, weight)])


def stacked(rows, fold):
    part = rows.shape[1] // fold
    return jnp.concatenate([rows[:, q * part : (q + 1) * part] for q in range(fold)], axis=0)


def turned(left, right):
    return lax.dot_general(left, right, (((0,), (0,)), ((), ())), preferred_element_type=F32)


def sum_of(parts_ref):
    total = parts_ref[0].astype(F32)
    for index in range(1, parts_ref.shape[0]):
        total = total + parts_ref[index].astype(F32)
    return total


def route_kernel(
    tok_rows, fold, parts_ref, gain_ref, router_ref, member_ref, placing_ref, out_ref, attended_ref
):
    width = gain_ref.shape[1]
    packed = sum_of(parts_ref)
    wide, places = folds(tok_rows, width)
    attended_ref[...] = jnp.zeros(attended_ref.shape, F32)
    attended_ref[:tok_rows, :wide] = packed[:tok_rows]
    for k, row, column in places:
        attended_ref[k : k + 1, wide:] = packed[row : row + 1, column : column + width - wide]
    attended = attended_ref[...]
    inverse = lax.rsqrt(jnp.mean(attended * attended, axis=1, keepdims=True) + 1e-05)
    normed = attended * inverse * gain_ref[...]
    logits = lax.dot_general(
        normed.astype(BF),
        router_ref[...],
        (((1,), (1,)), ((), ())),
        preferred_element_type=F32,
    )
    picked = jnp.sum(jnp.where(member_ref[...] > 0, logits, 0.0), axis=1, keepdims=True)
    routed = stacked(normed * jax.nn.sigmoid(picked), fold).astype(BF)
    out_ref[...] = jnp.dot(placing_ref[...], routed, preferred_element_type=F32).astype(BF)


def route(parts, gain, router_rows, member, placing, tok_rows, fold):
    whole = pl.BlockSpec(memory_space=pltpu.VMEM)
    width = gain.shape[1]
    return pl.pallas_call(
        functools.partial(route_kernel, tok_rows, fold),
        out_shape=jax.ShapeDtypeStruct((placing.shape[0], width // fold), BF),
        in_specs=[whole] * 5,
        out_specs=whole,
        scratch_shapes=[pltpu.VMEM((8, width), F32)],
        compiler_params=pltpu.CompilerParams(vmem_limit_bytes=8 << 20),
    )(parts, gain, router_rows, member, placing)


def compact_kernel(fold, cap, arrived_ref, out_ref, selector_ref):
    arrived = arrived_ref[...]
    rows = arrived.shape[0]
    square = (rows, rows)
    first = lax.broadcasted_iota(jnp.int32, square, 0)
    second = lax.broadcasted_iota(jnp.int32, square, 1)
    slot_first = lax.div(first, jnp.full(square, fold, jnp.int32))
    slot_second = lax.div(second, jnp.full(square, fold, jnp.int32))
    peak = jnp.max(jnp.abs(arrived.astype(F32)), axis=1, keepdims=True)
    filled = jnp.broadcast_to(jnp.where(peak > 0, 1.0, 0.0), (rows, LANES)).astype(BF)
    same = jnp.where(slot_first == slot_second, 1.0, 0.0).astype(BF)
    filled = jnp.dot(same, filled, preferred_element_type=F32) > 0
    heads = slot_second * fold == second
    before = jnp.where(heads & (slot_second < slot_first), 1.0, 0.0).astype(BF)
    ones = jnp.where(filled, 1.0, 0.0).astype(BF)
    position = jnp.dot(before, ones, preferred_element_type=F32).astype(jnp.int32)
    wide = (rows, LANES)
    row = lax.broadcasted_iota(jnp.int32, wide, 0)
    column = lax.broadcasted_iota(jnp.int32, wide, 1)
    piece = lax.div(column, jnp.full(wide, cap, jnp.int32))
    mine = lax.rem(row, jnp.full(wide, fold, jnp.int32)) == piece
    taken = filled & mine & (position == column - piece * cap)
    selector = jnp.where(taken, 1.0, 0.0).astype(BF)[:, : fold * cap]
    selector_ref[...] = selector
    compact = turned(selector, arrived)
    part = arrived.shape[1]
    for peer in range(out_ref.shape[0]):
        for q in range(fold):
            out_ref[peer, :, q * part : (q + 1) * part] = compact[
                q * cap : (q + 1) * cap
            ].astype(BF)


def compact_rows(arrived, fold, cap, peers):
    whole = pl.BlockSpec(memory_space=pltpu.VMEM)
    rows, part = arrived.shape
    return pl.pallas_call(
        functools.partial(compact_kernel, fold, cap),
        out_shape=(
            pltpu.VMEM((peers, cap, fold * part), BF),
            jax.ShapeDtypeStruct((rows, fold * cap), BF),
        ),
        in_specs=[whole],
        out_specs=(whole, whole),
        compiler_params=pltpu.CompilerParams(vmem_limit_bytes=8 << 20),
    )(arrived)


def return_kernel(fold, parts_ref, selector_ref, out_ref):
    expert_rows = stacked(sum_of(parts_ref), fold).astype(BF)
    out_ref[...] = jnp.dot(selector_ref[...], expert_rows, preferred_element_type=F32).astype(BF)


def combine_kernel(tok_rows, fold, returned_ref, placing_ref, out_ref):
    combined = turned(placing_ref[...], returned_ref[...])
    part = returned_ref.shape[1]
    rows = combined.shape[0] // fold
    for q in range(fold):
        out_ref[:, q * part : (q + 1) * part] = combined[q * rows : q * rows + tok_rows].astype(BF)


def combine(returned, placing, tok_rows, fold):
    whole = pl.BlockSpec(memory_space=pltpu.VMEM)
    return pl.pallas_call(
        functools.partial(combine_kernel, tok_rows, fold),
        out_shape=jax.ShapeDtypeStruct((tok_rows, fold * returned.shape[1]), BF),
        in_specs=[whole] * 2,
        out_specs=whole,
        compiler_params=pltpu.CompilerParams(vmem_limit_bytes=8 << 20),
    )(returned, placing)


def hidden_of(rows, gate_ref, up_ref):
    gate_value = jnp.dot(rows, gate_ref[...], preferred_element_type=F32)
    up_value = jnp.dot(rows, up_ref[...], preferred_element_type=F32)
    return (jax.nn.silu(gate_value) * up_value).astype(BF)


def expert_kernel(rows_ref, gate_ref, up_ref, down_ref, *refs):
    sources, out_ref, held, sems = refs[0:3], refs[3], refs[4:7], refs[7]
    copies = [
        pltpu.make_async_copy(source, target, sems.at[i])
        for i, (source, target) in enumerate(zip(sources, held))
    ]
    for copy in copies:
        copy.start()
    rows = rows_ref[...]
    first = hidden_of(rows, gate_ref, up_ref)
    copies[0].wait()
    copies[1].wait()
    second = hidden_of(rows, held[0], held[1])
    copies[2].wait()
    block = 1280
    for start in range(0, out_ref.shape[1], block):
        span = slice(start, start + block)
        total = jnp.dot(first, down_ref[:, span], preferred_element_type=F32)
        total = total + jnp.dot(second, held[2][:, span], preferred_element_type=F32)
        out_ref[:, span] = total.astype(BF)


def expert(rows, own, other):
    whole = pl.BlockSpec(memory_space=pltpu.VMEM)
    outside = pl.BlockSpec(memory_space=pl.ANY)
    return pl.pallas_call(
        expert_kernel,
        out_shape=pltpu.VMEM(rows.shape, BF),
        in_specs=[whole] * 4 + [outside] * 3,
        out_specs=whole,
        scratch_shapes=[pltpu.VMEM(weight.shape, BF) for weight in other]
        + [pltpu.SemaphoreType.DMA((3,))],
        compiler_params=pltpu.CompilerParams(vmem_limit_bytes=14 << 20),
    )(rows, *own, *[pltpu.with_memory_space_constraint(weight, pltpu.HBM) for weight in other])


def on_device(attn_heads, out_proj, norm_gain, router, expert_ids, w_gate, w_up, w_down):
    tensor_count = lax.axis_size("tensor")
    x_count = lax.axis_size("x")
    expert_axes = ("y", "w")
    expert_count = lax.axis_size(expert_axes)
    swap = [(0, 1), (1, 0)]
    head_rows = attn_heads.reshape(-1, attn_heads.shape[-1])
    tok_rows = head_rows.shape[0] // tensor_count
    width = out_proj.shape[1]
    send_cap = max(2, tok_rows // (expert_count // 2))
    recv_cap = min(tok_rows + max(2, tok_rows // 5), send_cap * (expert_count - 2) + 2)
    slots = expert_count * send_cap

    chosen_ids = expert_ids.reshape(-1)
    expert_index = jnp.arange(expert_count, dtype=jnp.int32)
    member = (chosen_ids[:, None] == expert_index[None, :]).astype(F32)
    same = chosen_ids[:, None] == chosen_ids[None, :]
    earlier = jnp.arange(tok_rows)[None, :] < jnp.arange(tok_rows)[:, None]
    rank_within = jnp.sum((same & earlier).astype(jnp.int32), axis=1)
    slot_index = chosen_ids * send_cap + rank_within
    spare = 8 - tok_rows
    fold = 8 // send_cap
    row_range = jnp.arange(slots * fold, dtype=jnp.int32)
    slot_columns = jnp.tile(jnp.pad(slot_index, (0, spare), constant_values=-1), fold)
    piece_columns = jnp.arange(fold * 8, dtype=jnp.int32) // 8
    target = jnp.where(slot_columns < 0, -1, slot_columns * fold + piece_columns)
    placing = (row_range[:, None] == target[None, :]).astype(BF)

    partial = project(head_rows, out_proj, tok_rows)
    parts = exchange(partial.reshape(tensor_count, 8, -1), "tensor")
    outgoing = route(
        parts,
        norm_gain[None],
        router.T,
        jnp.pad(member, ((0, spare), (0, 0))),
        placing,
        tok_rows,
        fold,
    )
    own = [w_gate[0], w_up[0], w_down[0]]
    outgoing, own = lax.optimization_barrier((outgoing, own))
    other = [lax.ppermute(weight, "core", swap) for weight in own]
    arrived = exchange(outgoing, expert_axes)
    arrived, own, other = lax.optimization_barrier((arrived, own, other))
    compact, selector = compact_rows(arrived, fold, recv_cap, tensor_count)
    rows = exchange(compact, "tensor").reshape(tensor_count * recv_cap, width)
    rows = spread(rows, "x").reshape(x_count * tensor_count * recv_cap, width)
    pair_sum = expert(rows, own, other)
    plane_sum = total_of(
        exchange(pair_sum.reshape(x_count, tensor_count * recv_cap, width), "x")
    ).astype(BF)
    parts = exchange(plane_sum.reshape(tensor_count, recv_cap, width), "tensor")
    back = local_call(
        functools.partial(return_kernel, fold),
        (slots * fold, width // fold),
        parts,
        selector,
    )
    returned = exchange(back, expert_axes)
    combined = combine(returned, placing, tok_rows, fold)
    return combined.reshape(1, tok_rows, 1, width)


def solution(mesh):
    dp, tensor, expert = (mesh.shape[name] for name in ("dp", "tensor", "expert"))
    fine = Mesh(
        mesh.devices.reshape(dp // 2, 2, tensor, expert // 3, 3), ("x", "core", "tensor", "y", "w")
    )
    dp_axes, expert_axes = ("x", "core"), ("y", "w")
    in_specs = (
        P(dp_axes, None, expert_axes, "tensor"),
        P("tensor", None),
        P(),
        P(),
        P(dp_axes, "tensor", expert_axes),
        P(expert_axes, None, (*dp_axes, "tensor")),
        P(expert_axes, None, (*dp_axes, "tensor")),
        P(expert_axes, (*dp_axes, "tensor"), None),
    )
    out_specs = P(dp_axes, "tensor", expert_axes, None)
    return jax.shard_map(
        on_device, mesh=fine, in_specs=in_specs, out_specs=out_specs, check_vma=False
    )
```

```python
import functools

import jax
import jax.numpy as jnp
from jax import lax
from jax.experimental import pallas as pl
from jax.experimental.pallas import tpu as pltpu
from jax.sharding import Mesh, PartitionSpec as P

BF = jnp.bfloat16
F32 = jnp.float32
LANES = 128
PIECES = 4


def exchange(value, axis):
    return lax.all_to_all(value, axis, split_axis=0, concat_axis=0, tiled=True)


def spread(value, axis):
    count = lax.axis_size(axis)
    return exchange(jnp.broadcast_to(value[None], (count,) + value.shape), axis)


def total_of(parts):
    total = parts[0].astype(F32)
    for index in range(1, parts.shape[0]):
        total = total + parts[index].astype(F32)
    return total


def in_vmem(value):
    return pltpu.with_memory_space_constraint(value, pltpu.VMEM)


def local_call(kernel, shape, *operands):
    whole = pl.BlockSpec(memory_space=pltpu.VMEM)
    return pl.pallas_call(
        kernel,
        out_shape=pltpu.VMEM(shape, BF),
        in_specs=[whole] * len(operands),
        out_specs=whole,
        compiler_params=pltpu.CompilerParams(vmem_limit_bytes=14 << 20),
    )(*operands)


def folds(tok_rows, width):
    wide = tok_rows * width // 8
    rest = width - wide
    each = wide // rest
    return wide, [(k, tok_rows + k // each, k % each * rest) for k in range(tok_rows)]


def project_kernel(chunks, tok_rows, source_ref, weight_ref, out_ref, heads_ref, held, packed, sems):
    depth = weight_ref.shape[0] // chunks
    width = weight_ref.shape[1]
    fetch = pltpu.make_async_copy(source_ref, heads_ref, sems.at[chunks * PIECES])
    fetch.start()
    copies = []
    for i in range(chunks * PIECES):
        rows = pl.ds(i * (depth // PIECES), depth // PIECES)
        copies.append(pltpu.make_async_copy(weight_ref.at[rows], held.at[rows], sems.at[i]))
        copies[i].start()
    fetch.wait()
    total = jnp.zeros((heads_ref.shape[0], width), F32)
    for i in range(chunks):
        for copy in copies[i * PIECES : (i + 1) * PIECES]:
            copy.wait()
        span = slice(i * depth, (i + 1) * depth)
        total = total + jnp.dot(heads_ref[:, span], held[span], preferred_element_type=F32)
    wide, places = folds(tok_rows, width)
    for peer in range(heads_ref.shape[0] // tok_rows):
        token = peer * tok_rows
        packed[8 * peer : 8 * peer + tok_rows] = total[token : token + tok_rows, :wide]
        for k, row, column in places:
            packed[8 * peer + row : 8 * peer + row + 1, column : column + width - wide] = total[
                token + k : token + k + 1, wide:
            ]
    out_ref[...] = packed[...].astype(BF)


def project(heads, weight, tok_rows):
    chunks = weight.shape[0] // LANES
    wide, _ = folds(tok_rows, weight.shape[1])
    packed_shape = (heads.shape[0] // tok_rows * 8, wide)
    whole = pl.BlockSpec(memory_space=pltpu.VMEM)
    return pl.pallas_call(
        functools.partial(project_kernel, chunks, tok_rows),
        out_shape=pltpu.VMEM(packed_shape, BF),
        in_specs=[pl.BlockSpec(memory_space=pl.ANY)] * 2,
        out_specs=whole,
        scratch_shapes=[
            pltpu.VMEM(heads.shape, BF),
            pltpu.VMEM(weight.shape, BF),
            pltpu.VMEM(packed_shape, F32),
            pltpu.SemaphoreType.DMA((chunks * PIECES + 1,)),
        ],
        compiler_params=pltpu.CompilerParams(vmem_limit_bytes=14 << 20),
    )(*[pltpu.with_memory_space_constraint(operand, pltpu.HBM) for operand in (heads, weight)])


def stacked(rows, fold):
    part = rows.shape[1] // fold
    return jnp.concatenate([rows[:, q * part : (q + 1) * part] for q in range(fold)], axis=0)


def turned(left, right):
    return lax.dot_general(left, right, (((0,), (0,)), ((), ())), preferred_element_type=F32)


def sum_of(parts_ref):
    total = parts_ref[0].astype(F32)
    for index in range(1, parts_ref.shape[0]):
        total = total + parts_ref[index].astype(F32)
    return total


def route_kernel(
    tok_rows, fold, parts_ref, gain_ref, router_ref, member_ref, placing_ref, out_ref, attended_ref
):
    width = gain_ref.shape[1]
    packed = sum_of(parts_ref)
    wide, places = folds(tok_rows, width)
    attended_ref[...] = jnp.zeros(attended_ref.shape, F32)
    attended_ref[:tok_rows, :wide] = packed[:tok_rows]
    for k, row, column in places:
        attended_ref[k : k + 1, wide:] = packed[row : row + 1, column : column + width - wide]
    attended = attended_ref[...]
    inverse = lax.rsqrt(jnp.mean(attended * attended, axis=1, keepdims=True) + 1e-05)
    normed = attended * inverse * gain_ref[...]
    logits = lax.dot_general(
        normed.astype(BF),
        router_ref[...],
        (((1,), (1,)), ((), ())),
        preferred_element_type=F32,
    )
    picked = jnp.sum(jnp.where(member_ref[...] > 0, logits, 0.0), axis=1, keepdims=True)
    routed = stacked(normed * jax.nn.sigmoid(picked), fold).astype(BF)
    out_ref[...] = jnp.dot(placing_ref[...], routed, preferred_element_type=F32).astype(BF)


def route(parts, gain, router_rows, member, placing, tok_rows, fold):
    whole = pl.BlockSpec(memory_space=pltpu.VMEM)
    width = gain.shape[1]
    return pl.pallas_call(
        functools.partial(route_kernel, tok_rows, fold),
        out_shape=jax.ShapeDtypeStruct((placing.shape[0], width // fold), BF),
        in_specs=[whole] * 5,
        out_specs=whole,
        scratch_shapes=[pltpu.VMEM((8, width), F32)],
        compiler_params=pltpu.CompilerParams(vmem_limit_bytes=8 << 20),
    )(parts, gain, router_rows, member, placing)


def compact_kernel(fold, cap, arrived_ref, out_ref, selector_ref):
    arrived = arrived_ref[...]
    rows = arrived.shape[0]
    square = (rows, rows)
    first = lax.broadcasted_iota(jnp.int32, square, 0)
    second = lax.broadcasted_iota(jnp.int32, square, 1)
    slot_first = lax.div(first, jnp.full(square, fold, jnp.int32))
    slot_second = lax.div(second, jnp.full(square, fold, jnp.int32))
    peak = jnp.max(jnp.abs(arrived.astype(F32)), axis=1, keepdims=True)
    filled = jnp.broadcast_to(jnp.where(peak > 0, 1.0, 0.0), (rows, LANES)).astype(BF)
    same = jnp.where(slot_first == slot_second, 1.0, 0.0).astype(BF)
    filled = jnp.dot(same, filled, preferred_element_type=F32) > 0
    heads = slot_second * fold == second
    before = jnp.where(heads & (slot_second < slot_first), 1.0, 0.0).astype(BF)
    ones = jnp.where(filled, 1.0, 0.0).astype(BF)
    position = jnp.dot(before, ones, preferred_element_type=F32).astype(jnp.int32)
    wide = (rows, LANES)
    row = lax.broadcasted_iota(jnp.int32, wide, 0)
    column = lax.broadcasted_iota(jnp.int32, wide, 1)
    piece = lax.div(column, jnp.full(wide, cap, jnp.int32))
    mine = lax.rem(row, jnp.full(wide, fold, jnp.int32)) == piece
    taken = filled & mine & (position == column - piece * cap)
    selector = jnp.where(taken, 1.0, 0.0).astype(BF)[:, : fold * cap]
    selector_ref[...] = selector
    compact = turned(selector, arrived)
    part = arrived.shape[1]
    for peer in range(out_ref.shape[0]):
        for q in range(fold):
            out_ref[peer, :, q * part : (q + 1) * part] = compact[
                q * cap : (q + 1) * cap
            ].astype(BF)


def compact_rows(arrived, fold, cap, peers):
    whole = pl.BlockSpec(memory_space=pltpu.VMEM)
    rows, part = arrived.shape
    return pl.pallas_call(
        functools.partial(compact_kernel, fold, cap),
        out_shape=(
            pltpu.VMEM((peers, cap, fold * part), BF),
            jax.ShapeDtypeStruct((rows, fold * cap), BF),
        ),
        in_specs=[whole],
        out_specs=(whole, whole),
        compiler_params=pltpu.CompilerParams(vmem_limit_bytes=8 << 20),
    )(arrived)


def return_kernel(fold, parts_ref, selector_ref, out_ref):
    expert_rows = stacked(sum_of(parts_ref), fold).astype(BF)
    out_ref[...] = jnp.dot(selector_ref[...], expert_rows, preferred_element_type=F32).astype(BF)


def combine_kernel(tok_rows, fold, returned_ref, placing_ref, out_ref):
    combined = turned(placing_ref[...], returned_ref[...])
    part = returned_ref.shape[1]
    rows = combined.shape[0] // fold
    for q in range(fold):
        out_ref[:, q * part : (q + 1) * part] = combined[q * rows : q * rows + tok_rows].astype(BF)


def combine(returned, placing, tok_rows, fold):
    whole = pl.BlockSpec(memory_space=pltpu.VMEM)
    return pl.pallas_call(
        functools.partial(combine_kernel, tok_rows, fold),
        out_shape=jax.ShapeDtypeStruct((tok_rows, fold * returned.shape[1]), BF),
        in_specs=[whole] * 2,
        out_specs=whole,
        compiler_params=pltpu.CompilerParams(vmem_limit_bytes=8 << 20),
    )(returned, placing)


def hidden_of(rows, gate_ref, up_ref):
    gate_value = jnp.dot(rows, gate_ref[...], preferred_element_type=F32)
    up_value = jnp.dot(rows, up_ref[...], preferred_element_type=F32)
    return (jax.nn.silu(gate_value) * up_value).astype(BF)


def expert_kernel(rows_ref, gate_ref, up_ref, down_ref, gate2_ref, up2_ref, source_ref, *refs):
    out_ref, down2_ref, sem = refs
    fetch = pltpu.make_async_copy(source_ref, down2_ref, sem)
    fetch.start()
    rows = rows_ref[...]
    first = hidden_of(rows, gate_ref, up_ref)
    second = hidden_of(rows, gate2_ref, up2_ref)
    fetch.wait()
    block = 1280
    for start in range(0, out_ref.shape[1], block):
        span = slice(start, start + block)
        total = jnp.dot(first, down_ref[:, span], preferred_element_type=F32)
        total = total + jnp.dot(second, down2_ref[:, span], preferred_element_type=F32)
        out_ref[:, span] = total.astype(BF)


def expert(rows, own, other):
    whole = pl.BlockSpec(memory_space=pltpu.VMEM)
    down = pltpu.with_memory_space_constraint(other[2], pltpu.HBM)
    return pl.pallas_call(
        expert_kernel,
        out_shape=pltpu.VMEM(rows.shape, BF),
        in_specs=[whole] * 6 + [pl.BlockSpec(memory_space=pl.ANY)],
        out_specs=whole,
        scratch_shapes=[pltpu.VMEM(down.shape, BF), pltpu.SemaphoreType.DMA],
        compiler_params=pltpu.CompilerParams(vmem_limit_bytes=14 << 20),
    )(rows, *own, *other[:2], down)


def on_device(attn_heads, out_proj, norm_gain, router, expert_ids, w_gate, w_up, w_down):
    tensor_count = lax.axis_size("tensor")
    x_count = lax.axis_size("x")
    expert_axes = ("y", "w")
    expert_count = lax.axis_size(expert_axes)
    swap = [(0, 1), (1, 0)]
    head_rows = attn_heads.reshape(-1, attn_heads.shape[-1])
    tok_rows = head_rows.shape[0] // tensor_count
    width = out_proj.shape[1]
    send_cap = max(2, tok_rows // (expert_count // 2))
    recv_cap = min(tok_rows + max(2, tok_rows // 5), send_cap * (expert_count - 2) + 2)
    slots = expert_count * send_cap

    chosen_ids = expert_ids.reshape(-1)
    expert_index = jnp.arange(expert_count, dtype=jnp.int32)
    member = (chosen_ids[:, None] == expert_index[None, :]).astype(F32)
    same = chosen_ids[:, None] == chosen_ids[None, :]
    earlier = jnp.arange(tok_rows)[None, :] < jnp.arange(tok_rows)[:, None]
    rank_within = jnp.sum((same & earlier).astype(jnp.int32), axis=1)
    slot_index = chosen_ids * send_cap + rank_within
    spare = 8 - tok_rows
    fold = 8 // send_cap
    row_range = jnp.arange(slots * fold, dtype=jnp.int32)
    slot_columns = jnp.tile(jnp.pad(slot_index, (0, spare), constant_values=-1), fold)
    piece_columns = jnp.arange(fold * 8, dtype=jnp.int32) // 8
    target = jnp.where(slot_columns < 0, -1, slot_columns * fold + piece_columns)
    placing = (row_range[:, None] == target[None, :]).astype(BF)

    partial = project(head_rows, out_proj, tok_rows)
    parts = exchange(partial.reshape(tensor_count, 8, -1), "tensor")
    outgoing = route(
        parts,
        norm_gain[None],
        router.T,
        jnp.pad(member, ((0, spare), (0, 0))),
        placing,
        tok_rows,
        fold,
    )
    own = [w_gate[0], w_up[0], w_down[0]]
    outgoing, own = lax.optimization_barrier((outgoing, own))
    other = [lax.ppermute(weight, "core", swap) for weight in own]
    arrived = exchange(outgoing, expert_axes)
    arrived, own, other = lax.optimization_barrier((arrived, own, other))
    compact, selector = compact_rows(arrived, fold, recv_cap, tensor_count)
    rows = exchange(compact, "tensor").reshape(tensor_count * recv_cap, width)
    rows = spread(rows, "x").reshape(x_count * tensor_count * recv_cap, width)
    pair_sum = expert(rows, own, other)
    plane_sum = total_of(
        exchange(pair_sum.reshape(x_count, tensor_count * recv_cap, width), "x")
    ).astype(BF)
    parts = exchange(plane_sum.reshape(tensor_count, recv_cap, width), "tensor")
    back = local_call(
        functools.partial(return_kernel, fold),
        (slots * fold, width // fold),
        parts,
        selector,
    )
    returned = exchange(back, expert_axes)
    combined = combine(returned, placing, tok_rows, fold)
    return combined.reshape(1, tok_rows, 1, width)


def solution(mesh):
    dp, tensor, expert = (mesh.shape[name] for name in ("dp", "tensor", "expert"))
    fine = Mesh(
        mesh.devices.reshape(dp // 2, 2, tensor, expert // 3, 3), ("x", "core", "tensor", "y", "w")
    )
    dp_axes, expert_axes = ("x", "core"), ("y", "w")
    in_specs = (
        P(dp_axes, None, expert_axes, "tensor"),
        P("tensor", None),
        P(),
        P(),
        P(dp_axes, "tensor", expert_axes),
        P(expert_axes, None, (*dp_axes, "tensor")),
        P(expert_axes, None, (*dp_axes, "tensor")),
        P(expert_axes, (*dp_axes, "tensor"), None),
    )
    out_specs = P(dp_axes, "tensor", expert_axes, None)
    return jax.shard_map(
        on_device, mesh=fine, in_specs=in_specs, out_specs=out_specs, check_vma=False
    )
```

```python
import functools

import jax
import jax.numpy as jnp
from jax import lax
from jax.experimental import pallas as pl
from jax.experimental.pallas import tpu as pltpu
from jax.sharding import Mesh, PartitionSpec as P

BF = jnp.bfloat16
F32 = jnp.float32
LANES = 128
PIECE = 64


def exchange(value, axis):
    return lax.all_to_all(value, axis, split_axis=0, concat_axis=0, tiled=True)


def spread(value, axis):
    count = lax.axis_size(axis)
    return exchange(jnp.broadcast_to(value[None], (count,) + value.shape), axis)


def total_of(parts):
    total = parts[0].astype(F32)
    for index in range(1, parts.shape[0]):
        total = total + parts[index].astype(F32)
    return total


def in_vmem(value):
    return pltpu.with_memory_space_constraint(value, pltpu.VMEM)


def local_call(kernel, shape, *operands):
    whole = pl.BlockSpec(memory_space=pltpu.VMEM)
    return pl.pallas_call(
        kernel,
        out_shape=pltpu.VMEM(shape, BF),
        in_specs=[whole] * len(operands),
        out_specs=whole,
        compiler_params=pltpu.CompilerParams(vmem_limit_bytes=14 << 20),
    )(*operands)


def folds(tok_rows, width):
    wide = tok_rows * width // 8
    rest = width - wide
    each = wide // rest
    return wide, [(k, tok_rows + k // each, k % each * rest) for k in range(tok_rows)]


def start_copies(source_ref, target_ref, sems, piece):
    copies = []
    for i in range(source_ref.shape[0] // piece):
        rows = pl.ds(i * piece, piece)
        copies.append(pltpu.make_async_copy(source_ref.at[rows], target_ref.at[rows], sems.at[i]))
        copies[i].start()
    return copies


def project_kernel(tok_rows, source_ref, weight_ref, out_ref, heads_ref, held, packed, sem, sems):
    depth, width = weight_ref.shape
    fetch = pltpu.make_async_copy(source_ref, heads_ref, sem)
    fetch.start()
    copies = start_copies(weight_ref, held, sems, PIECE)
    fetch.wait()
    total = None
    for start in range(0, depth, 256):
        stop = min(start + 256, depth)
        for copy in copies[start // PIECE : stop // PIECE]:
            copy.wait()
        part = jnp.dot(heads_ref[:, start:stop], held[start:stop], preferred_element_type=F32)
        total = part if total is None else total + part
    wide, places = folds(tok_rows, width)
    for peer in range(heads_ref.shape[0] // tok_rows):
        token = peer * tok_rows
        packed[8 * peer : 8 * peer + tok_rows] = total[token : token + tok_rows, :wide]
        for k, row, column in places:
            packed[8 * peer + row : 8 * peer + row + 1, column : column + width - wide] = total[
                token + k : token + k + 1, wide:
            ]
    out_ref[...] = packed[...].astype(BF)


def project(heads, weight, tok_rows):
    wide, _ = folds(tok_rows, weight.shape[1])
    packed_shape = (heads.shape[0] // tok_rows * 8, wide)
    whole = pl.BlockSpec(memory_space=pltpu.VMEM)
    return pl.pallas_call(
        functools.partial(project_kernel, tok_rows),
        out_shape=pltpu.VMEM(packed_shape, BF),
        in_specs=[pl.BlockSpec(memory_space=pl.ANY)] * 2,
        out_specs=whole,
        scratch_shapes=[
            pltpu.VMEM(heads.shape, BF),
            pltpu.VMEM(weight.shape, BF),
            pltpu.VMEM(packed_shape, F32),
            pltpu.SemaphoreType.DMA,
            pltpu.SemaphoreType.DMA((weight.shape[0] // PIECE,)),
        ],
        compiler_params=pltpu.CompilerParams(vmem_limit_bytes=14 << 20),
    )(*[pltpu.with_memory_space_constraint(operand, pltpu.HBM) for operand in (heads, weight)])


def stacked(rows, fold):
    part = rows.shape[1] // fold
    return jnp.concatenate([rows[:, q * part : (q + 1) * part] for q in range(fold)], axis=0)


def turned(left, right):
    return lax.dot_general(left, right, (((0,), (0,)), ((), ())), preferred_element_type=F32)


def sum_of(parts_ref):
    total = parts_ref[0].astype(F32)
    for index in range(1, parts_ref.shape[0]):
        total = total + parts_ref[index].astype(F32)
    return total


def route_kernel(
    tok_rows, fold, parts_ref, gain_ref, router_ref, member_ref, placing_ref, out_ref, attended_ref
):
    width = gain_ref.shape[1]
    packed = sum_of(parts_ref)
    wide, places = folds(tok_rows, width)
    attended_ref[...] = jnp.zeros(attended_ref.shape, F32)
    attended_ref[:tok_rows, :wide] = packed[:tok_rows]
    for k, row, column in places:
        attended_ref[k : k + 1, wide:] = packed[row : row + 1, column : column + width - wide]
    attended = attended_ref[...]
    inverse = lax.rsqrt(jnp.mean(attended * attended, axis=1, keepdims=True) + 1e-05)
    normed = attended * inverse * gain_ref[...]
    logits = lax.dot_general(
        normed.astype(BF),
        router_ref[...],
        (((1,), (1,)), ((), ())),
        preferred_element_type=F32,
    )
    picked = jnp.sum(jnp.where(member_ref[...] > 0, logits, 0.0), axis=1, keepdims=True)
    routed = stacked(normed * jax.nn.sigmoid(picked), fold).astype(BF)
    out_ref[...] = jnp.dot(placing_ref[...], routed, preferred_element_type=F32).astype(BF)


def route(parts, gain, router_rows, member, placing, tok_rows, fold):
    whole = pl.BlockSpec(memory_space=pltpu.VMEM)
    width = gain.shape[1]
    return pl.pallas_call(
        functools.partial(route_kernel, tok_rows, fold),
        out_shape=jax.ShapeDtypeStruct((placing.shape[0], width // fold), BF),
        in_specs=[whole] * 5,
        out_specs=whole,
        scratch_shapes=[pltpu.VMEM((8, width), F32)],
        compiler_params=pltpu.CompilerParams(vmem_limit_bytes=8 << 20),
    )(parts, gain, router_rows, member, placing)


def compact_kernel(fold, cap, arrived_ref, out_ref, selector_ref):
    arrived = arrived_ref[...]
    rows = arrived.shape[0]
    square = (rows, rows)
    first = lax.broadcasted_iota(jnp.int32, square, 0)
    second = lax.broadcasted_iota(jnp.int32, square, 1)
    slot_first = lax.div(first, jnp.full(square, fold, jnp.int32))
    slot_second = lax.div(second, jnp.full(square, fold, jnp.int32))
    peak = jnp.max(jnp.abs(arrived.astype(F32)), axis=1, keepdims=True)
    filled = jnp.broadcast_to(jnp.where(peak > 0, 1.0, 0.0), (rows, LANES)).astype(BF)
    same = jnp.where(slot_first == slot_second, 1.0, 0.0).astype(BF)
    filled = jnp.dot(same, filled, preferred_element_type=F32) > 0
    heads = slot_second * fold == second
    before = jnp.where(heads & (slot_second < slot_first), 1.0, 0.0).astype(BF)
    ones = jnp.where(filled, 1.0, 0.0).astype(BF)
    position = jnp.dot(before, ones, preferred_element_type=F32).astype(jnp.int32)
    wide = (rows, LANES)
    row = lax.broadcasted_iota(jnp.int32, wide, 0)
    column = lax.broadcasted_iota(jnp.int32, wide, 1)
    piece = lax.div(column, jnp.full(wide, cap, jnp.int32))
    mine = lax.rem(row, jnp.full(wide, fold, jnp.int32)) == piece
    taken = filled & mine & (position == column - piece * cap)
    selector = jnp.where(taken, 1.0, 0.0).astype(BF)[:, : fold * cap]
    selector_ref[...] = selector
    compact = turned(selector, arrived)
    part = arrived.shape[1]
    for peer in range(out_ref.shape[0]):
        for q in range(fold):
            out_ref[peer, :, q * part : (q + 1) * part] = compact[
                q * cap : (q + 1) * cap
            ].astype(BF)


def compact_rows(arrived, fold, cap, peers):
    whole = pl.BlockSpec(memory_space=pltpu.VMEM)
    rows, part = arrived.shape
    return pl.pallas_call(
        functools.partial(compact_kernel, fold, cap),
        out_shape=(
            pltpu.VMEM((peers, cap, fold * part), BF),
            jax.ShapeDtypeStruct((rows, fold * cap), BF),
        ),
        in_specs=[whole],
        out_specs=(whole, whole),
        compiler_params=pltpu.CompilerParams(vmem_limit_bytes=8 << 20),
    )(arrived)


def return_kernel(fold, parts_ref, selector_ref, out_ref):
    expert_rows = stacked(sum_of(parts_ref), fold).astype(BF)
    out_ref[...] = jnp.dot(selector_ref[...], expert_rows, preferred_element_type=F32).astype(BF)


def combine_kernel(tok_rows, fold, returned_ref, placing_ref, out_ref):
    combined = turned(placing_ref[...], returned_ref[...])
    part = returned_ref.shape[1]
    rows = combined.shape[0] // fold
    for q in range(fold):
        out_ref[:, q * part : (q + 1) * part] = combined[q * rows : q * rows + tok_rows].astype(BF)


def combine(returned, placing, tok_rows, fold):
    whole = pl.BlockSpec(memory_space=pltpu.VMEM)
    return pl.pallas_call(
        functools.partial(combine_kernel, tok_rows, fold),
        out_shape=jax.ShapeDtypeStruct((tok_rows, fold * returned.shape[1]), BF),
        in_specs=[whole] * 2,
        out_specs=whole,
        compiler_params=pltpu.CompilerParams(vmem_limit_bytes=8 << 20),
    )(returned, placing)


def hidden_of(rows, gate_ref, up_ref):
    gate_value = jnp.dot(rows, gate_ref[...], preferred_element_type=F32)
    up_value = jnp.dot(rows, up_ref[...], preferred_element_type=F32)
    return (jax.nn.silu(gate_value) * up_value).astype(BF)


def expert_kernel(rows_ref, gate_ref, up_ref, down_ref, gate2_ref, up2_ref, source_ref, *refs):
    out_ref, down2_ref, sems = refs
    copies = start_copies(source_ref, down2_ref, sems, 16)
    rows = rows_ref[...]
    first = hidden_of(rows, gate_ref, up_ref)
    second = hidden_of(rows, gate2_ref, up2_ref)
    for copy in copies:
        copy.wait()
    block = 1280
    for start in range(0, out_ref.shape[1], block):
        span = slice(start, start + block)
        total = jnp.dot(first, down_ref[:, span], preferred_element_type=F32)
        total = total + jnp.dot(second, down2_ref[:, span], preferred_element_type=F32)
        out_ref[:, span] = total.astype(BF)


def expert(rows, own, other):
    whole = pl.BlockSpec(memory_space=pltpu.VMEM)
    down = pltpu.with_memory_space_constraint(other[2], pltpu.HBM)
    return pl.pallas_call(
        expert_kernel,
        out_shape=pltpu.VMEM(rows.shape, BF),
        in_specs=[whole] * 6 + [pl.BlockSpec(memory_space=pl.ANY)],
        out_specs=whole,
        scratch_shapes=[
            pltpu.VMEM(down.shape, BF),
            pltpu.SemaphoreType.DMA((down.shape[0] // 16,)),
        ],
        compiler_params=pltpu.CompilerParams(vmem_limit_bytes=14 << 20),
    )(rows, *own, *other[:2], down)


def on_device(attn_heads, out_proj, norm_gain, router, expert_ids, w_gate, w_up, w_down):
    tensor_count = lax.axis_size("tensor")
    x_count = lax.axis_size("x")
    expert_axes = ("y", "w")
    expert_count = lax.axis_size(expert_axes)
    swap = [(0, 1), (1, 0)]
    head_rows = attn_heads.reshape(-1, attn_heads.shape[-1])
    tok_rows = head_rows.shape[0] // tensor_count
    width = out_proj.shape[1]
    send_cap = max(2, tok_rows // (expert_count // 2))
    recv_cap = min(tok_rows + max(2, tok_rows // 5), send_cap * (expert_count - 2) + 2)
    slots = expert_count * send_cap

    chosen_ids = expert_ids.reshape(-1)
    expert_index = jnp.arange(expert_count, dtype=jnp.int32)
    member = (chosen_ids[:, None] == expert_index[None, :]).astype(F32)
    same = chosen_ids[:, None] == chosen_ids[None, :]
    earlier = jnp.arange(tok_rows)[None, :] < jnp.arange(tok_rows)[:, None]
    rank_within = jnp.sum((same & earlier).astype(jnp.int32), axis=1)
    slot_index = chosen_ids * send_cap + rank_within
    spare = 8 - tok_rows
    fold = 8 // send_cap
    row_range = jnp.arange(slots * fold, dtype=jnp.int32)
    slot_columns = jnp.tile(jnp.pad(slot_index, (0, spare), constant_values=-1), fold)
    piece_columns = jnp.arange(fold * 8, dtype=jnp.int32) // 8
    target = jnp.where(slot_columns < 0, -1, slot_columns * fold + piece_columns)
    placing = (row_range[:, None] == target[None, :]).astype(BF)

    partial = project(head_rows, out_proj, tok_rows)
    parts = exchange(partial.reshape(tensor_count, 8, -1), "tensor")
    outgoing = route(
        parts,
        norm_gain[None],
        router.T,
        jnp.pad(member, ((0, spare), (0, 0))),
        placing,
        tok_rows,
        fold,
    )
    own = [w_gate[0], w_up[0], w_down[0]]
    outgoing, own = lax.optimization_barrier((outgoing, own))
    other = [lax.ppermute(weight, "core", swap) for weight in own]
    arrived = exchange(outgoing, expert_axes)
    arrived, own, other = lax.optimization_barrier((arrived, own, other))
    compact, selector = compact_rows(arrived, fold, recv_cap, tensor_count)
    rows = exchange(compact, "tensor").reshape(tensor_count * recv_cap, width)
    rows = spread(rows, "x").reshape(x_count * tensor_count * recv_cap, width)
    pair_sum = expert(rows, own, other)
    plane_sum = total_of(
        exchange(pair_sum.reshape(x_count, tensor_count * recv_cap, width), "x")
    ).astype(BF)
    parts = exchange(plane_sum.reshape(tensor_count, recv_cap, width), "tensor")
    back = local_call(
        functools.partial(return_kernel, fold),
        (slots * fold, width // fold),
        parts,
        selector,
    )
    returned = exchange(back, expert_axes)
    combined = combine(returned, placing, tok_rows, fold)
    return combined.reshape(1, tok_rows, 1, width)


def solution(mesh):
    dp, tensor, expert = (mesh.shape[name] for name in ("dp", "tensor", "expert"))
    fine = Mesh(
        mesh.devices.reshape(dp // 2, 2, tensor, expert // 3, 3), ("x", "core", "tensor", "y", "w")
    )
    dp_axes, expert_axes = ("x", "core"), ("y", "w")
    in_specs = (
        P(dp_axes, None, expert_axes, "tensor"),
        P("tensor", None),
        P(),
        P(),
        P(dp_axes, "tensor", expert_axes),
        P(expert_axes, None, (*dp_axes, "tensor")),
        P(expert_axes, None, (*dp_axes, "tensor")),
        P(expert_axes, (*dp_axes, "tensor"), None),
    )
    out_specs = P(dp_axes, "tensor", expert_axes, None)
    return jax.shard_map(
        on_device, mesh=fine, in_specs=in_specs, out_specs=out_specs, check_vma=False
    )
```

```python
import functools

import jax
import jax.numpy as jnp
from jax import lax
from jax.experimental import pallas as pl
from jax.experimental.pallas import tpu as pltpu
from jax.sharding import Mesh, PartitionSpec as P

BF = jnp.bfloat16
F32 = jnp.float32
LANES = 128
PIECES = 4
BLOCK = 1280


def exchange(value, axis):
    return lax.all_to_all(value, axis, split_axis=0, concat_axis=0, tiled=True)


def spread(value, axis):
    count = lax.axis_size(axis)
    return exchange(jnp.broadcast_to(value[None], (count,) + value.shape), axis)


def total_of(parts):
    total = parts[0].astype(F32)
    for index in range(1, parts.shape[0]):
        total = total + parts[index].astype(F32)
    return total


def in_vmem(value):
    return pltpu.with_memory_space_constraint(value, pltpu.VMEM)


def local_call(kernel, shape, *operands):
    whole = pl.BlockSpec(memory_space=pltpu.VMEM)
    return pl.pallas_call(
        kernel,
        out_shape=pltpu.VMEM(shape, BF),
        in_specs=[whole] * len(operands),
        out_specs=whole,
        compiler_params=pltpu.CompilerParams(vmem_limit_bytes=14 << 20),
    )(*operands)


def folds(tok_rows, width):
    wide = tok_rows * width // 8
    rest = width - wide
    each = wide // rest
    return wide, [(k, tok_rows + k // each, k % each * rest) for k in range(tok_rows)]


def project_kernel(chunks, tok_rows, source_ref, weight_ref, out_ref, heads_ref, held, packed, sems):
    depth = weight_ref.shape[0] // chunks
    width = weight_ref.shape[1]
    fetch = pltpu.make_async_copy(source_ref, heads_ref, sems.at[chunks * PIECES])
    fetch.start()
    copies = []
    for i in range(chunks * PIECES):
        rows = pl.ds(i * (depth // PIECES), depth // PIECES)
        copies.append(pltpu.make_async_copy(weight_ref.at[rows], held.at[rows], sems.at[i]))
        copies[i].start()
    fetch.wait()
    total = jnp.zeros((heads_ref.shape[0], width), F32)
    for i in range(chunks):
        for copy in copies[i * PIECES : (i + 1) * PIECES]:
            copy.wait()
        span = slice(i * depth, (i + 1) * depth)
        total = total + jnp.dot(heads_ref[:, span], held[span], preferred_element_type=F32)
    wide, places = folds(tok_rows, width)
    for peer in range(heads_ref.shape[0] // tok_rows):
        token = peer * tok_rows
        packed[8 * peer : 8 * peer + tok_rows] = total[token : token + tok_rows, :wide]
        for k, row, column in places:
            packed[8 * peer + row : 8 * peer + row + 1, column : column + width - wide] = total[
                token + k : token + k + 1, wide:
            ]
    out_ref[...] = packed[...].astype(BF)


def project(heads, weight, tok_rows):
    chunks = weight.shape[0] // LANES
    wide, _ = folds(tok_rows, weight.shape[1])
    packed_shape = (heads.shape[0] // tok_rows * 8, wide)
    whole = pl.BlockSpec(memory_space=pltpu.VMEM)
    return pl.pallas_call(
        functools.partial(project_kernel, chunks, tok_rows),
        out_shape=pltpu.VMEM(packed_shape, BF),
        in_specs=[pl.BlockSpec(memory_space=pl.ANY)] * 2,
        out_specs=whole,
        scratch_shapes=[
            pltpu.VMEM(heads.shape, BF),
            pltpu.VMEM(weight.shape, BF),
            pltpu.VMEM(packed_shape, F32),
            pltpu.SemaphoreType.DMA((chunks * PIECES + 1,)),
        ],
        compiler_params=pltpu.CompilerParams(vmem_limit_bytes=14 << 20),
    )(*[pltpu.with_memory_space_constraint(operand, pltpu.HBM) for operand in (heads, weight)])


def stacked(rows, fold):
    part = rows.shape[1] // fold
    return jnp.concatenate([rows[:, q * part : (q + 1) * part] for q in range(fold)], axis=0)


def turned(left, right):
    return lax.dot_general(left, right, (((0,), (0,)), ((), ())), preferred_element_type=F32)


def sum_of(parts_ref):
    total = parts_ref[0].astype(F32)
    for index in range(1, parts_ref.shape[0]):
        total = total + parts_ref[index].astype(F32)
    return total


def route_kernel(
    tok_rows, fold, parts_ref, gain_ref, router_ref, member_ref, placing_ref, out_ref, attended_ref
):
    width = gain_ref.shape[1]
    packed = sum_of(parts_ref)
    wide, places = folds(tok_rows, width)
    attended_ref[...] = jnp.zeros(attended_ref.shape, F32)
    attended_ref[:tok_rows, :wide] = packed[:tok_rows]
    for k, row, column in places:
        attended_ref[k : k + 1, wide:] = packed[row : row + 1, column : column + width - wide]
    attended = attended_ref[...]
    inverse = lax.rsqrt(jnp.mean(attended * attended, axis=1, keepdims=True) + 1e-05)
    normed = attended * inverse * gain_ref[...]
    logits = lax.dot_general(
        normed.astype(BF),
        router_ref[...],
        (((1,), (1,)), ((), ())),
        preferred_element_type=F32,
    )
    picked = jnp.sum(jnp.where(member_ref[...] > 0, logits, 0.0), axis=1, keepdims=True)
    routed = stacked(normed * jax.nn.sigmoid(picked), fold).astype(BF)
    out_ref[...] = jnp.dot(placing_ref[...], routed, preferred_element_type=F32).astype(BF)


def route(parts, gain, router_rows, member, placing, tok_rows, fold):
    whole = pl.BlockSpec(memory_space=pltpu.VMEM)
    width = gain.shape[1]
    return pl.pallas_call(
        functools.partial(route_kernel, tok_rows, fold),
        out_shape=jax.ShapeDtypeStruct((placing.shape[0], width // fold), BF),
        in_specs=[whole] * 5,
        out_specs=whole,
        scratch_shapes=[pltpu.VMEM((8, width), F32)],
        compiler_params=pltpu.CompilerParams(vmem_limit_bytes=8 << 20),
    )(parts, gain, router_rows, member, placing)


def compact_kernel(fold, cap, arrived_ref, out_ref, selector_ref):
    arrived = arrived_ref[...]
    rows = arrived.shape[0]
    square = (rows, rows)
    first = lax.broadcasted_iota(jnp.int32, square, 0)
    second = lax.broadcasted_iota(jnp.int32, square, 1)
    slot_first = lax.div(first, jnp.full(square, fold, jnp.int32))
    slot_second = lax.div(second, jnp.full(square, fold, jnp.int32))
    peak = jnp.max(jnp.abs(arrived.astype(F32)), axis=1, keepdims=True)
    filled = jnp.broadcast_to(jnp.where(peak > 0, 1.0, 0.0), (rows, LANES)).astype(BF)
    same = jnp.where(slot_first == slot_second, 1.0, 0.0).astype(BF)
    filled = jnp.dot(same, filled, preferred_element_type=F32) > 0
    heads = slot_second * fold == second
    before = jnp.where(heads & (slot_second < slot_first), 1.0, 0.0).astype(BF)
    ones = jnp.where(filled, 1.0, 0.0).astype(BF)
    position = jnp.dot(before, ones, preferred_element_type=F32).astype(jnp.int32)
    wide = (rows, LANES)
    row = lax.broadcasted_iota(jnp.int32, wide, 0)
    column = lax.broadcasted_iota(jnp.int32, wide, 1)
    piece = lax.div(column, jnp.full(wide, cap, jnp.int32))
    mine = lax.rem(row, jnp.full(wide, fold, jnp.int32)) == piece
    taken = filled & mine & (position == column - piece * cap)
    selector = jnp.where(taken, 1.0, 0.0).astype(BF)[:, : fold * cap]
    selector_ref[...] = selector
    compact = turned(selector, arrived)
    part = arrived.shape[1]
    for peer in range(out_ref.shape[0]):
        for q in range(fold):
            out_ref[peer, :, q * part : (q + 1) * part] = compact[
                q * cap : (q + 1) * cap
            ].astype(BF)


def compact_rows(arrived, fold, cap, peers):
    whole = pl.BlockSpec(memory_space=pltpu.VMEM)
    rows, part = arrived.shape
    return pl.pallas_call(
        functools.partial(compact_kernel, fold, cap),
        out_shape=(
            pltpu.VMEM((peers, cap, fold * part), BF),
            jax.ShapeDtypeStruct((rows, fold * cap), BF),
        ),
        in_specs=[whole],
        out_specs=(whole, whole),
        compiler_params=pltpu.CompilerParams(vmem_limit_bytes=8 << 20),
    )(arrived)


def return_kernel(fold, parts_ref, selector_ref, out_ref):
    expert_rows = stacked(sum_of(parts_ref), fold).astype(BF)
    out_ref[...] = jnp.dot(selector_ref[...], expert_rows, preferred_element_type=F32).astype(BF)


def combine_kernel(tok_rows, fold, returned_ref, placing_ref, out_ref):
    combined = turned(placing_ref[...], returned_ref[...])
    part = returned_ref.shape[1]
    rows = combined.shape[0] // fold
    for q in range(fold):
        out_ref[:, q * part : (q + 1) * part] = combined[q * rows : q * rows + tok_rows].astype(BF)


def combine(returned, placing, tok_rows, fold):
    whole = pl.BlockSpec(memory_space=pltpu.VMEM)
    return pl.pallas_call(
        functools.partial(combine_kernel, tok_rows, fold),
        out_shape=jax.ShapeDtypeStruct((tok_rows, fold * returned.shape[1]), BF),
        in_specs=[whole] * 2,
        out_specs=whole,
        compiler_params=pltpu.CompilerParams(vmem_limit_bytes=8 << 20),
    )(returned, placing)


def hidden_of(rows, gate_ref, up_ref):
    gate_value = jnp.dot(rows, gate_ref[...], preferred_element_type=F32)
    up_value = jnp.dot(rows, up_ref[...], preferred_element_type=F32)
    return (jax.nn.silu(gate_value) * up_value).astype(BF)


def expert_kernel(rows_ref, gate_ref, up_ref, down_ref, gate2_ref, up2_ref, source_ref, *refs):
    out_ref, down2_ref, sems = refs
    spans = [pl.ds(i * BLOCK, BLOCK) for i in range(out_ref.shape[1] // BLOCK)]
    copies = [
        pltpu.make_async_copy(source_ref.at[:, span], down2_ref.at[:, span], sems.at[i])
        for i, span in enumerate(spans)
    ]
    for copy in copies:
        copy.start()
    rows = rows_ref[...]
    first = hidden_of(rows, gate_ref, up_ref)
    second = hidden_of(rows, gate2_ref, up2_ref)
    for copy, span in zip(copies, spans):
        total = jnp.dot(first, down_ref[:, span], preferred_element_type=F32)
        copy.wait()
        total = total + jnp.dot(second, down2_ref[:, span], preferred_element_type=F32)
        out_ref[:, span] = total.astype(BF)


def expert(rows, own, other):
    whole = pl.BlockSpec(memory_space=pltpu.VMEM)
    down = pltpu.with_memory_space_constraint(other[2], pltpu.HBM)
    return pl.pallas_call(
        expert_kernel,
        out_shape=pltpu.VMEM(rows.shape, BF),
        in_specs=[whole] * 6 + [pl.BlockSpec(memory_space=pl.ANY)],
        out_specs=whole,
        scratch_shapes=[
            pltpu.VMEM(down.shape, BF),
            pltpu.SemaphoreType.DMA((down.shape[1] // BLOCK,)),
        ],
        compiler_params=pltpu.CompilerParams(vmem_limit_bytes=14 << 20),
    )(rows, *own, *other[:2], down)


def on_device(attn_heads, out_proj, norm_gain, router, expert_ids, w_gate, w_up, w_down):
    tensor_count = lax.axis_size("tensor")
    x_count = lax.axis_size("x")
    expert_axes = ("y", "w")
    expert_count = lax.axis_size(expert_axes)
    swap = [(0, 1), (1, 0)]
    head_rows = attn_heads.reshape(-1, attn_heads.shape[-1])
    tok_rows = head_rows.shape[0] // tensor_count
    width = out_proj.shape[1]
    send_cap = max(2, tok_rows // (expert_count // 2))
    recv_cap = min(tok_rows + max(2, tok_rows // 5), send_cap * (expert_count - 2) + 2)
    slots = expert_count * send_cap

    chosen_ids = expert_ids.reshape(-1)
    expert_index = jnp.arange(expert_count, dtype=jnp.int32)
    member = (chosen_ids[:, None] == expert_index[None, :]).astype(F32)
    same = chosen_ids[:, None] == chosen_ids[None, :]
    earlier = jnp.arange(tok_rows)[None, :] < jnp.arange(tok_rows)[:, None]
    rank_within = jnp.sum((same & earlier).astype(jnp.int32), axis=1)
    slot_index = chosen_ids * send_cap + rank_within
    spare = 8 - tok_rows
    fold = 8 // send_cap
    row_range = jnp.arange(slots * fold, dtype=jnp.int32)
    slot_columns = jnp.tile(jnp.pad(slot_index, (0, spare), constant_values=-1), fold)
    piece_columns = jnp.arange(fold * 8, dtype=jnp.int32) // 8
    target = jnp.where(slot_columns < 0, -1, slot_columns * fold + piece_columns)
    placing = (row_range[:, None] == target[None, :]).astype(BF)

    partial = project(head_rows, out_proj, tok_rows)
    parts = exchange(partial.reshape(tensor_count, 8, -1), "tensor")
    outgoing = route(
        parts,
        norm_gain[None],
        router.T,
        jnp.pad(member, ((0, spare), (0, 0))),
        placing,
        tok_rows,
        fold,
    )
    own = [w_gate[0], w_up[0], w_down[0]]
    outgoing, own = lax.optimization_barrier((outgoing, own))
    other = [lax.ppermute(weight, "core", swap) for weight in own]
    arrived = exchange(outgoing, expert_axes)
    arrived, own, other = lax.optimization_barrier((arrived, own, other))
    compact, selector = compact_rows(arrived, fold, recv_cap, tensor_count)
    rows = exchange(compact, "tensor").reshape(tensor_count * recv_cap, width)
    rows = spread(rows, "x").reshape(x_count * tensor_count * recv_cap, width)
    pair_sum = expert(rows, own, other)
    plane_sum = total_of(
        exchange(pair_sum.reshape(x_count, tensor_count * recv_cap, width), "x")
    ).astype(BF)
    parts = exchange(plane_sum.reshape(tensor_count, recv_cap, width), "tensor")
    back = local_call(
        functools.partial(return_kernel, fold),
        (slots * fold, width // fold),
        parts,
        selector,
    )
    returned = exchange(back, expert_axes)
    combined = combine(returned, placing, tok_rows, fold)
    return combined.reshape(1, tok_rows, 1, width)


def solution(mesh):
    dp, tensor, expert = (mesh.shape[name] for name in ("dp", "tensor", "expert"))
    fine = Mesh(
        mesh.devices.reshape(dp // 2, 2, tensor, expert // 3, 3), ("x", "core", "tensor", "y", "w")
    )
    dp_axes, expert_axes = ("x", "core"), ("y", "w")
    in_specs = (
        P(dp_axes, None, expert_axes, "tensor"),
        P("tensor", None),
        P(),
        P(),
        P(dp_axes, "tensor", expert_axes),
        P(expert_axes, None, (*dp_axes, "tensor")),
        P(expert_axes, None, (*dp_axes, "tensor")),
        P(expert_axes, (*dp_axes, "tensor"), None),
    )
    out_specs = P(dp_axes, "tensor", expert_axes, None)
    return jax.shard_map(
        on_device, mesh=fine, in_specs=in_specs, out_specs=out_specs, check_vma=False
    )
```

```python
import functools

import jax
import jax.numpy as jnp
from jax import lax
from jax.experimental import pallas as pl
from jax.experimental.pallas import tpu as pltpu
from jax.sharding import Mesh, PartitionSpec as P

BF = jnp.bfloat16
F32 = jnp.float32
LANES = 128
PIECES = 4


def exchange(value, axis):
    return lax.all_to_all(value, axis, split_axis=0, concat_axis=0, tiled=True)


def spread(value, axis):
    count = lax.axis_size(axis)
    return exchange(jnp.broadcast_to(value[None], (count,) + value.shape), axis)


def total_of(parts):
    total = parts[0].astype(F32)
    for index in range(1, parts.shape[0]):
        total = total + parts[index].astype(F32)
    return total


def in_vmem(value):
    return pltpu.with_memory_space_constraint(value, pltpu.VMEM)


def local_call(kernel, shape, *operands):
    whole = pl.BlockSpec(memory_space=pltpu.VMEM)
    return pl.pallas_call(
        kernel,
        out_shape=pltpu.VMEM(shape, BF),
        in_specs=[whole] * len(operands),
        out_specs=whole,
        compiler_params=pltpu.CompilerParams(vmem_limit_bytes=14 << 20),
    )(*operands)


def folds(tok_rows, width):
    wide = tok_rows * width // 8
    rest = width - wide
    each = wide // rest
    return wide, [(k, tok_rows + k // each, k % each * rest) for k in range(tok_rows)]


def project_kernel(chunks, tok_rows, source_ref, weight_ref, out_ref, heads_ref, held, packed, sems):
    depth = weight_ref.shape[0] // chunks
    width = weight_ref.shape[1]
    fetch = pltpu.make_async_copy(source_ref, heads_ref, sems.at[chunks * PIECES])
    fetch.start()
    copies = []
    for i in range(chunks * PIECES):
        rows = pl.ds(i * (depth // PIECES), depth // PIECES)
        copies.append(pltpu.make_async_copy(weight_ref.at[rows], held.at[rows], sems.at[i]))
        copies[i].start()
    fetch.wait()
    total = jnp.zeros((heads_ref.shape[0], width), F32)
    for i in range(chunks):
        for copy in copies[i * PIECES : (i + 1) * PIECES]:
            copy.wait()
        span = slice(i * depth, (i + 1) * depth)
        total = total + jnp.dot(heads_ref[:, span], held[span], preferred_element_type=F32)
    wide, places = folds(tok_rows, width)
    for peer in range(heads_ref.shape[0] // tok_rows):
        token = peer * tok_rows
        packed[8 * peer : 8 * peer + tok_rows] = total[token : token + tok_rows, :wide]
        for k, row, column in places:
            packed[8 * peer + row : 8 * peer + row + 1, column : column + width - wide] = total[
                token + k : token + k + 1, wide:
            ]
    out_ref[...] = packed[...].astype(BF)


def project(heads, weight, tok_rows):
    chunks = weight.shape[0] // LANES
    wide, _ = folds(tok_rows, weight.shape[1])
    packed_shape = (heads.shape[0] // tok_rows * 8, wide)
    whole = pl.BlockSpec(memory_space=pltpu.VMEM)
    return pl.pallas_call(
        functools.partial(project_kernel, chunks, tok_rows),
        out_shape=pltpu.VMEM(packed_shape, BF),
        in_specs=[pl.BlockSpec(memory_space=pl.ANY)] * 2,
        out_specs=whole,
        scratch_shapes=[
            pltpu.VMEM(heads.shape, BF),
            pltpu.VMEM(weight.shape, BF),
            pltpu.VMEM(packed_shape, F32),
            pltpu.SemaphoreType.DMA((chunks * PIECES + 1,)),
        ],
        compiler_params=pltpu.CompilerParams(vmem_limit_bytes=14 << 20),
    )(*[pltpu.with_memory_space_constraint(operand, pltpu.HBM) for operand in (heads, weight)])


def stacked(rows, fold):
    part = rows.shape[1] // fold
    return jnp.concatenate([rows[:, q * part : (q + 1) * part] for q in range(fold)], axis=0)


def turned(left, right):
    return lax.dot_general(left, right, (((0,), (0,)), ((), ())), preferred_element_type=F32)


def sum_of(parts_ref):
    total = parts_ref[0].astype(F32)
    for index in range(1, parts_ref.shape[0]):
        total = total + parts_ref[index].astype(F32)
    return total


def route_kernel(
    tok_rows, fold, parts_ref, gain_ref, router_ref, member_ref, placing_ref, out_ref, attended_ref
):
    width = gain_ref.shape[1]
    packed = sum_of(parts_ref)
    wide, places = folds(tok_rows, width)
    attended_ref[...] = jnp.zeros(attended_ref.shape, F32)
    attended_ref[:tok_rows, :wide] = packed[:tok_rows]
    for k, row, column in places:
        attended_ref[k : k + 1, wide:] = packed[row : row + 1, column : column + width - wide]
    attended = attended_ref[...]
    inverse = lax.rsqrt(jnp.mean(attended * attended, axis=1, keepdims=True) + 1e-05)
    normed = attended * inverse * gain_ref[...]
    logits = lax.dot_general(
        normed.astype(BF),
        router_ref[...],
        (((1,), (1,)), ((), ())),
        preferred_element_type=F32,
    )
    picked = jnp.sum(jnp.where(member_ref[...] > 0, logits, 0.0), axis=1, keepdims=True)
    routed = stacked(normed * jax.nn.sigmoid(picked), fold).astype(BF)
    out_ref[...] = jnp.dot(placing_ref[...], routed, preferred_element_type=F32).astype(BF)


def route(parts, gain, router_rows, member, placing, tok_rows, fold):
    whole = pl.BlockSpec(memory_space=pltpu.VMEM)
    width = gain.shape[1]
    return pl.pallas_call(
        functools.partial(route_kernel, tok_rows, fold),
        out_shape=jax.ShapeDtypeStruct((placing.shape[0], width // fold), BF),
        in_specs=[whole] * 5,
        out_specs=whole,
        scratch_shapes=[pltpu.VMEM((8, width), F32)],
        compiler_params=pltpu.CompilerParams(vmem_limit_bytes=8 << 20),
    )(parts, gain, router_rows, member, placing)


def compact_kernel(fold, cap, arrived_ref, out_ref, selector_ref):
    arrived = arrived_ref[...]
    rows = arrived.shape[0]
    square = (rows, rows)
    first = lax.broadcasted_iota(jnp.int32, square, 0)
    second = lax.broadcasted_iota(jnp.int32, square, 1)
    slot_first = lax.div(first, jnp.full(square, fold, jnp.int32))
    slot_second = lax.div(second, jnp.full(square, fold, jnp.int32))
    peak = jnp.max(jnp.abs(arrived.astype(F32)), axis=1, keepdims=True)
    filled = jnp.broadcast_to(jnp.where(peak > 0, 1.0, 0.0), (rows, LANES)).astype(BF)
    same = jnp.where(slot_first == slot_second, 1.0, 0.0).astype(BF)
    filled = jnp.dot(same, filled, preferred_element_type=F32) > 0
    heads = slot_second * fold == second
    before = jnp.where(heads & (slot_second < slot_first), 1.0, 0.0).astype(BF)
    ones = jnp.where(filled, 1.0, 0.0).astype(BF)
    position = jnp.dot(before, ones, preferred_element_type=F32).astype(jnp.int32)
    wide = (rows, LANES)
    row = lax.broadcasted_iota(jnp.int32, wide, 0)
    column = lax.broadcasted_iota(jnp.int32, wide, 1)
    piece = lax.div(column, jnp.full(wide, cap, jnp.int32))
    mine = lax.rem(row, jnp.full(wide, fold, jnp.int32)) == piece
    taken = filled & mine & (position == column - piece * cap)
    selector = jnp.where(taken, 1.0, 0.0).astype(BF)[:, : fold * cap]
    selector_ref[...] = selector
    compact = turned(selector, arrived)
    part = arrived.shape[1]
    for peer in range(out_ref.shape[0]):
        for q in range(fold):
            out_ref[peer, :, q * part : (q + 1) * part] = compact[
                q * cap : (q + 1) * cap
            ].astype(BF)


def compact_rows(arrived, fold, cap, peers):
    whole = pl.BlockSpec(memory_space=pltpu.VMEM)
    rows, part = arrived.shape
    return pl.pallas_call(
        functools.partial(compact_kernel, fold, cap),
        out_shape=(
            pltpu.VMEM((peers, cap, fold * part), BF),
            jax.ShapeDtypeStruct((rows, fold * cap), BF),
        ),
        in_specs=[whole],
        out_specs=(whole, whole),
        compiler_params=pltpu.CompilerParams(vmem_limit_bytes=8 << 20),
    )(arrived)


def return_kernel(fold, parts_ref, selector_ref, out_ref):
    expert_rows = stacked(sum_of(parts_ref), fold).astype(BF)
    out_ref[...] = jnp.dot(selector_ref[...], expert_rows, preferred_element_type=F32).astype(BF)


def combine_kernel(tok_rows, fold, returned_ref, placing_ref, out_ref):
    combined = turned(placing_ref[...], returned_ref[...])
    part = returned_ref.shape[1]
    rows = combined.shape[0] // fold
    for q in range(fold):
        out_ref[:, q * part : (q + 1) * part] = combined[q * rows : q * rows + tok_rows].astype(BF)


def combine(returned, placing, tok_rows, fold):
    whole = pl.BlockSpec(memory_space=pltpu.VMEM)
    return pl.pallas_call(
        functools.partial(combine_kernel, tok_rows, fold),
        out_shape=jax.ShapeDtypeStruct((tok_rows, fold * returned.shape[1]), BF),
        in_specs=[whole] * 2,
        out_specs=whole,
        compiler_params=pltpu.CompilerParams(vmem_limit_bytes=8 << 20),
    )(returned, placing)


def hidden_of(rows, gate_ref, up_ref):
    gate_value = jnp.dot(rows, gate_ref[...], preferred_element_type=F32)
    up_value = jnp.dot(rows, up_ref[...], preferred_element_type=F32)
    return (jax.nn.silu(gate_value) * up_value).astype(BF)


def expert_kernel(
    rows_ref, gate_ref, up_ref, down_ref, gate2_ref, up2_ref, down2_ref, out_ref
):
    rows = rows_ref[...]
    first = hidden_of(rows, gate_ref, up_ref)
    second = hidden_of(rows, gate2_ref, up2_ref)
    block = 1280
    for start in range(0, out_ref.shape[1], block):
        span = slice(start, start + block)
        total = jnp.dot(first, down_ref[:, span], preferred_element_type=F32)
        total = total + jnp.dot(second, down2_ref[:, span], preferred_element_type=F32)
        out_ref[:, span] = total.astype(BF)


def on_device(attn_heads, out_proj, norm_gain, router, expert_ids, w_gate, w_up, w_down):
    tensor_count = lax.axis_size("tensor")
    x_count = lax.axis_size("x")
    expert_axes = ("y", "w")
    expert_count = lax.axis_size(expert_axes)
    swap = [(0, 1), (1, 0)]
    head_rows = attn_heads.reshape(-1, attn_heads.shape[-1])
    tok_rows = head_rows.shape[0] // tensor_count
    width = out_proj.shape[1]
    send_cap = max(2, tok_rows // (expert_count // 2))
    recv_cap = min(tok_rows + max(2, tok_rows // 5), send_cap * (expert_count - 2) + 2)
    slots = expert_count * send_cap

    chosen_ids = expert_ids.reshape(-1)
    expert_index = jnp.arange(expert_count, dtype=jnp.int32)
    member = (chosen_ids[:, None] == expert_index[None, :]).astype(F32)
    same = chosen_ids[:, None] == chosen_ids[None, :]
    earlier = jnp.arange(tok_rows)[None, :] < jnp.arange(tok_rows)[:, None]
    rank_within = jnp.sum((same & earlier).astype(jnp.int32), axis=1)
    slot_index = chosen_ids * send_cap + rank_within
    spare = 8 - tok_rows
    fold = 8 // send_cap
    row_range = jnp.arange(slots * fold, dtype=jnp.int32)
    slot_columns = jnp.tile(jnp.pad(slot_index, (0, spare), constant_values=-1), fold)
    piece_columns = jnp.arange(fold * 8, dtype=jnp.int32) // 8
    target = jnp.where(slot_columns < 0, -1, slot_columns * fold + piece_columns)
    placing = (row_range[:, None] == target[None, :]).astype(BF)

    partial = project(head_rows, out_proj, tok_rows)
    parts = exchange(partial.reshape(tensor_count, 8, -1), "tensor")
    outgoing = route(
        parts,
        norm_gain[None],
        router.T,
        jnp.pad(member, ((0, spare), (0, 0))),
        placing,
        tok_rows,
        fold,
    )
    own = [w_gate[0], w_up[0], w_down[0]]
    outgoing, own = lax.optimization_barrier((outgoing, own))
    other = [lax.ppermute(weight, "core", swap) for weight in own]
    arrived = exchange(outgoing, expert_axes)
    arrived, own, other = lax.optimization_barrier((arrived, own, other))
    compact, selector = compact_rows(arrived, fold, recv_cap, tensor_count)
    rows = exchange(compact, "tensor").reshape(tensor_count * recv_cap, width)
    rows = spread(rows, "x").reshape(x_count * tensor_count * recv_cap, width)
    pair_sum = local_call(expert_kernel, rows.shape, rows, *own, *other)
    plane_sum = total_of(
        exchange(pair_sum.reshape(x_count, tensor_count * recv_cap, width), "x")
    ).astype(BF)
    parts = exchange(plane_sum.reshape(tensor_count, recv_cap, width), "tensor")
    back = local_call(
        functools.partial(return_kernel, fold),
        (slots * fold, width // fold),
        parts,
        selector,
    )
    returned = exchange(back, expert_axes)
    combined = combine(returned, placing, tok_rows, fold)
    return combined.reshape(1, tok_rows, 1, width)


def solution(mesh):
    dp, tensor, expert = (mesh.shape[name] for name in ("dp", "tensor", "expert"))
    fine = Mesh(
        mesh.devices.reshape(dp // 2, 2, tensor, expert // 3, 3), ("x", "core", "tensor", "y", "w")
    )
    dp_axes, expert_axes = ("x", "core"), ("y", "w")
    in_specs = (
        P(dp_axes, None, expert_axes, "tensor"),
        P("tensor", None),
        P(),
        P(),
        P(dp_axes, "tensor", expert_axes),
        P(expert_axes, None, (*dp_axes, "tensor")),
        P(expert_axes, None, (*dp_axes, "tensor")),
        P(expert_axes, (*dp_axes, "tensor"), None),
    )
    out_specs = P(dp_axes, "tensor", expert_axes, None)
    return jax.shard_map(
        on_device, mesh=fine, in_specs=in_specs, out_specs=out_specs, check_vma=False
    )
```
